256 devices in a mesh: row: 8 (over y, core), col: 32 (over x, z).
Axes of the slice: x: 4, y: 4, z: 8, core: 2. Of those that a mesh axis runs over, the one named last changes fastest.
Arguments:
- features: bfloat16 [262144, 256], P(('row', 'col')), may hold values from -12 to 12
- grad_out: bfloat16 [262144, 256], P(('row', 'col')), may hold values from -12 to 12
- conv_weight: bfloat16 [27, 256, 256], replicated, may hold values from -0.078125 to 0.078125
- pool_gain: float32 [5, 256], replicated, may hold values from -4 to 4
- neighbours: int32 [27, 262144], P(None, ('row', 'col')), may hold values from 0 to 1536, as said below
- requests: int32 [8192, 16], P(('row', 'col')), may hold values from 0 to 1023, as said below
- pool_mask: int32 [5, 262144], P(None, ('row', 'col')), may hold values 0 or 1
Outputs:
- feature_grad: bfloat16 [262144, 256], P(('row', 'col'))
- weight_grad: float32 [27, 256, 256], replicated
- gain_grad: float32 [5, 256], replicated
The draws below stay inside these ranges and needn't reach their ends.
Inputs may be any that keep to these rules, and one draw needn't show every extreme that they name: `neighbours`: entry 13 of an octant is the octant itself. Toward each peer p of its row a device uses a prefix of its 16 ghost slots p * 16 .. p * 16 + n - 1: none toward itself, all 16 toward at least one peer, and every used slot is named by some octant. `requests`: unused slots also hold valid octant numbers of the peer.
All inputs are finite; a program needn't handle non-finite values. No bound on the sum of `pool_mask` on one device may be relied on, other than what follows from the above.
Results may differ from the reference program's by a relative error of at most 0.0045.
Values may be sent and summed in bfloat16 or wider, within the bound.
A program may use at most 128 MiB of HBM per device.

```python
import math
import jax
import jax.numpy as jnp
from jax import lax

C = 256
ROWS = 1024
BUCKET = 16
LEV = 5
TOTAL = 262144
GHOSTS = 512
N_COL = 32
DEVICES = 256


def ghost_counts(key):
    key = jax.random.fold_in(key, 7)
    first, second = jax.random.split(key)
    columns = jnp.arange(N_COL, dtype=jnp.int32)[None, :]
    own_col = (jnp.arange(DEVICES, dtype=jnp.int32) % N_COL)[:, None]
    counts = jax.random.randint(first, (DEVICES, N_COL), BUCKET // 4, BUCKET + 1, dtype=jnp.int32)
    fullest = (own_col + 1 + jax.random.randint(second, (DEVICES, 1), 0, N_COL - 1, dtype=jnp.int32)) % N_COL
    counts = jnp.where(columns == fullest, BUCKET, counts)
    return jnp.where(columns == own_col, 0, counts)


def draw_neighbours(key, part):
    counts = ghost_counts(key)
    key = jax.random.fold_in(key, 11)
    keys = jax.random.split(key, 3)
    ends = jnp.cumsum(counts, axis=1)
    starts = ends - counts
    live = ends[:, -1]
    ranks = jnp.arange(GHOSTS, dtype=jnp.int32)
    peer_of = jnp.sum((ranks[None, :, None] >= ends[:, None, :]).astype(jnp.int32), axis=2)
    peer_safe = jnp.minimum(peer_of, N_COL - 1)
    offsets = ranks[None, :] - jnp.take_along_axis(starts, peer_safe, axis=1)
    slot_table = peer_safe * BUCKET + offsets
    kinds = jax.random.randint(keys[0], (DEVICES, ROWS, 27), 0, 20, dtype=jnp.int32)
    local_rows = jax.random.randint(keys[1], (DEVICES, ROWS, 27), 0, ROWS, dtype=jnp.int32)
    picks = jax.random.randint(keys[2], (DEVICES, ROWS, 27), 0, 1 << 20, dtype=jnp.int32) % live[:, None, None]
    row_ids = jnp.arange(ROWS, dtype=jnp.int32)[None, :, None]
    tap_ids = jnp.arange(27, dtype=jnp.int32)[None, None, :]
    first_use = jnp.logical_and(tap_ids == 0, row_ids < live[:, None, None])
    picks = jnp.where(first_use, row_ids, picks)
    ghost_rows = ROWS + jnp.take_along_axis(slot_table, picks.reshape(DEVICES, ROWS * 27), axis=1).reshape(DEVICES, ROWS, 27)
    chosen = jnp.where(kinds < 2, ROWS + GHOSTS, jnp.where(kinds < 7, ghost_rows, local_rows))
    chosen = jnp.where(first_use, ghost_rows, chosen)
    chosen = jnp.where(tap_ids == 13, row_ids, chosen)
    return jnp.transpose(chosen, (2, 0, 1)).reshape(27, DEVICES * ROWS).astype(jnp.int32)


def draw_requests(key, part):
    key = jax.random.fold_in(key, 13)
    return jax.random.randint(key, (DEVICES * N_COL, BUCKET), 0, ROWS, dtype=jnp.int32)


def draw_features(key, part):
    key = jax.random.fold_in(key, 17)
    first, second = jax.random.split(key, 2)
    col_scale = jnp.exp(jax.random.uniform(first, (1, C), jnp.float32, math.log(0.3), math.log(3.0)))
    base = jnp.clip(jax.random.normal(second, (TOTAL, C), jnp.float32), -4.0, 4.0)
    return (base * col_scale).astype(jnp.bfloat16)


def draw_grad_out(key, part):
    key = jax.random.fold_in(key, 19)
    first, second = jax.random.split(key, 2)
    col_scale = jnp.exp(jax.random.uniform(first, (1, C), jnp.float32, math.log(0.3), math.log(3.0)))
    base = jnp.clip(jax.random.normal(second, (TOTAL, C), jnp.float32), -4.0, 4.0)
    return (base * col_scale).astype(jnp.bfloat16)


def place_ends(entries, rng, least, top_value):
    dims = entries.shape
    index_at = [jax.random.randint(jax.random.fold_in(rng, axis), (), 0, dims[axis]) for axis in range(len(dims))]
    entries = entries.at[tuple(index_at)].set(least)
    longest = dims.index(max(dims))
    index_at[longest] = (index_at[longest] + 1) % dims[longest]
    return entries.at[tuple(index_at)].set(top_value)


def noise(stream_key, shape, scale, limit, kind=jnp.bfloat16):
    drawn = jax.random.normal(stream_key, shape, jnp.float32) * scale
    return jnp.minimum(jnp.maximum(drawn, -limit), limit).astype(kind)


def setup_inputs(seed: int = 0) -> dict:
    streams_of = jax.random.split(jax.random.key(seed), 8)
    features = draw_features(jax.random.fold_in(streams_of[7], 71), 0)
    grad_out = draw_grad_out(jax.random.fold_in(streams_of[7], 71), 0)
    conv_weight = noise(streams_of[2], (27, C, C), (27 * C) ** -0.5, 0.078125)
    pool_gain = noise(streams_of[3], (LEV, C), 1.0, 4.0, jnp.float32)
    neighbours = draw_neighbours(jax.random.fold_in(streams_of[7], 71), 0)
    requests = draw_requests(jax.random.fold_in(streams_of[7], 71), 0)
    pool_mask = place_ends((jax.random.randint(streams_of[6], (LEV, TOTAL), 0, 2) < 1).astype(jnp.int32), jax.random.fold_in(streams_of[6], 1), 0, 1)
    return {"features": features, "grad_out": grad_out, "conv_weight": conv_weight, "pool_gain": pool_gain, "neighbours": neighbours, "requests": requests, "pool_mask": pool_mask}


clip_norm = 1024.0
tiny_eps = 1e-06

def reference(features, grad_out, conv_weight, pool_gain, neighbours, requests, pool_mask):
    row_device = jnp.arange(TOTAL, dtype=jnp.int32) // ROWS
    device_grid = jnp.broadcast_to(row_device[None, :], neighbours.shape)
    is_local = neighbours < ROWS
    is_ghost = jnp.logical_and(neighbours >= ROWS, neighbours < ROWS + GHOSTS)
    slot_index = jnp.clip(neighbours - ROWS, 0, GHOSTS - 1)
    peer_col = slot_index // BUCKET
    slot_pos = slot_index % BUCKET
    owner_dev = device_grid // N_COL * N_COL + peer_col
    source_row = requests[device_grid * N_COL + peer_col, slot_pos]
    global_source = jnp.where(is_local, device_grid * ROWS + neighbours, jnp.where(is_ghost, owner_dev * ROWS + source_row, TOTAL)).astype(jnp.int32)
    padded_feat = jnp.concatenate([features, jnp.zeros((1, C), jnp.bfloat16)], axis=0)

    def one_tap(grad_rows, inputs):
        tap_index, tap_weight = inputs
        gathered = padded_feat[tap_index]
        tap_grad = lax.dot_general(gathered, grad_out, (((0,), (0,)), ((), ())), preferred_element_type=jnp.float32)
        spread = lax.dot_general(grad_out, tap_weight, (((1,), (1,)), ((), ())), preferred_element_type=jnp.float32)
        return (grad_rows.at[tap_index].add(spread), tap_grad)
    grad_rows, weight_raw = lax.scan(one_tap, jnp.zeros((TOTAL + 1, C), jnp.float32), (global_source, conv_weight))
    mask_float = pool_mask.astype(jnp.float32).reshape(LEV, DEVICES, ROWS)
    grad_float = grad_out.astype(jnp.float32).reshape(DEVICES, ROWS, C)
    feat_float = features.astype(jnp.float32).reshape(DEVICES, ROWS, C)
    level_sums = jnp.einsum('ldr,drc->ldc', mask_float, grad_float, precision=lax.Precision.HIGHEST)
    feature_sums = jnp.einsum('ldr,drc->ldc', mask_float, feat_float, precision=lax.Precision.HIGHEST)
    pooled_parts = []
    for level_index in range(LEV):
        group_size = 2 ** (level_index + 1)
        stride = DEVICES // group_size
        grouped = level_sums[level_index].reshape(group_size, stride, C).sum(axis=0)
        pooled_parts.append(jnp.tile(grouped, (group_size, 1)) * (2.0 ** (level_index + 1) * ROWS) ** (-0.5))
    pooled = jnp.stack(pooled_parts)
    pool_term = jnp.einsum('ldr,ldc->drc', mask_float, pooled * pool_gain[:, None, :], precision=lax.Precision.HIGHEST).reshape(TOTAL, C)
    feature_grad = (grad_rows[:TOTAL] + pool_term).astype(jnp.bfloat16)
    gain_raw = lax.optimization_barrier(jnp.sum(feature_sums * pooled, axis=1))
    grad_norm = jnp.sqrt(jnp.sum(weight_raw * weight_raw) + jnp.sum(gain_raw * gain_raw) + tiny_eps)
    factor = jnp.minimum(1.0, clip_norm / grad_norm)
    return (feature_grad, weight_raw * factor, gain_raw * factor)
```

```python
import jax
import jax.numpy as jnp
from jax import lax
from jax.experimental import pallas as pl
from jax.experimental.pallas import tpu as pltpu
from jax.sharding import PartitionSpec as P

MESH = pl.DeviceIdType.MESH
clip_norm = 1024.0
tiny_eps = 1e-06
ROWS = 1024
C = 256
TAPS = 27
BUCKET = 16
PEERS = 32
GHOSTS = PEERS * BUCKET
SLOTS = ROWS + GHOSTS
LEV = 5
T = 4
NG = 28 // T
R = T * C
HALF = R // 2
QUARTER = HALF // 4
PIECE = HALF // 16
AHEAD = 2
LAST_H = NG - AHEAD
STEPS = NG + 7
f32 = jnp.float32
bf16 = jnp.bfloat16


def wait_for(ref, sem):
    pltpu.make_async_copy(ref, ref, sem).wait()


def whole(
    features_ref,
    grad_ref,
    neighbours_ref,
    requests_ref,
    mask_ref,
    gain_ref,
    weight_hbm,
    fgrad_ref,
    wsum_ref,
    gain_out,
    scale_out,
    spread,
    ext_t,
    wpart,
    r0,
    a1,
    r1,
    a2,
    r2,
    r3,
    weight,
    total,
    wanted,
    owner_t,
    outgoing,
    ghosts,
    terms,
    returned,
    maskf,
    gainf,
    level_out,
    level_in,
    pooled,
    gains0,
    gains_y,
    gains_x,
    gains_z,
    squares,
    send,
    recv,
    halo_send,
    halo_recv,
    level_send,
    level_recv,
    gain_send,
    gain_recv,
    weight_sem,
):
    row = lax.axis_index("row")
    col = lax.axis_index("col")
    y = row // 2
    core = row % 2
    x = col // 8
    z = col % 8

    def push(src, dst, send_sem, recv_sem, device):
        pltpu.make_async_remote_copy(
            src_ref=src,
            dst_ref=dst,
            send_sem=send_sem,
            recv_sem=recv_sem,
            device_id=device,
            device_id_type=MESH,
        ).start()

    weight_copy = pltpu.make_async_copy(weight_hbm, weight, weight_sem)
    weight_copy.start()

    barrier = pltpu.get_barrier_semaphore()

    def greet(offset, carry):
        pl.semaphore_signal(
            barrier, inc=1, device_id=(row, (col + offset) % PEERS), device_id_type=MESH
        )
        return carry

    lax.fori_loop(1, PEERS, greet, 0)
    pl.semaphore_signal(barrier, inc=1, device_id=(y * 2 + 1 - core, col), device_id_type=MESH)
    for offset in range(1, 4):
        pl.semaphore_signal(
            barrier, inc=1, device_id=((y + offset) % 4 * 2 + core, col), device_id_type=MESH
        )

    maskf[...] = jnp.zeros_like(maskf)
    maskf[0:LEV, :] = mask_ref[...].astype(f32)
    gainf[...] = jnp.zeros_like(gainf)
    gainf[0:LEV, :] = gain_ref[...]
    level_out[0] = jnp.dot(maskf[...].astype(bf16), grad_ref[...], preferred_element_type=f32)
    wanted[pl.ds(col, 1)] = jnp.zeros((1, 1, 128), jnp.int32)
    own = pl.ds(pl.multiple_of(col * BUCKET, BUCKET), BUCKET)
    ghosts[own, :] = jnp.zeros((BUCKET, C), bf16)
    returned[own, :] = jnp.zeros((BUCKET, C), bf16)
    wpart[TAPS * C :, :] = jnp.zeros(((NG * T - TAPS) * C, C), f32)
    squares[...] = jnp.zeros_like(squares)
    total[...] = jnp.zeros_like(total)

    pl.semaphore_wait(barrier, PEERS - 1 + 1 + 3)

    def ask(offset, carry):
        peer = (col + offset) % PEERS
        push(requests_ref.at[peer], wanted.at[col], halo_send.at[0], halo_recv.at[0], (row, peer))
        return carry

    lax.fori_loop(1, PEERS, ask, 0)

    level_partner = (
        ((y + 2) % 4 * 2 + core, col),
        ((y + 1 - 2 * (y % 2)) * 2 + core, col),
        (y * 2 + 1 - core, col),
        (row, (x + 2) % 4 * 8 + z),
        (row, (x + 1 - 2 * (x % 2)) * 8 + z),
    )

    def level_start(level):
        push(
            level_out.at[level],
            level_in.at[level],
            level_send.at[level],
            level_recv.at[level],
            level_partner[level],
        )

    level_rows = lax.broadcasted_iota(jnp.int32, (8, C), 0)

    def level_end(level):
        wait_for(level_in.at[level], level_recv.at[level])
        summed = level_out[level] + jnp.where(level_rows >= level, level_in[level], 0.0)
        if level < LEV - 1:
            level_out[level + 1] = summed
            level_start(level + 1)
            return
        scale = jnp.zeros((8, C), f32)
        for row_level in range(LEV):
            value = (2.0 ** (row_level + 1) * ROWS) ** (-0.5)
            scale = jnp.where(level_rows == row_level, value, scale)
        pooled[...] = summed * scale
        feature_sums = jnp.dot(
            maskf[...].astype(bf16), features_ref[...], preferred_element_type=f32
        )
        gains0[0] = feature_sums * pooled[...]
        push(
            gains0.at[0], gains0.at[1], gain_send.at[0], gain_recv.at[0], (y * 2 + 1 - core, col)
        )

    def gain_stage(stage):
        if stage == 1:
            wait_for(gains0.at[1], gain_recv.at[0])
            gains_y[pl.ds(y, 1)] = (gains0[0] + gains0[1])[None]
            for offset in range(1, 4):
                device = ((y + offset) % 4 * 2 + core, col)
                push(gains_y.at[y], gains_y.at[y], gain_send.at[1], gain_recv.at[1], device)
        elif stage == 2:
            wait_for(gains_y.at[0:3], gain_recv.at[1])
            gains_x[pl.ds(x, 1)] = jnp.sum(gains_y[...], axis=0, keepdims=True)
            for offset in range(1, 4):
                device = (row, (x + offset) % 4 * 8 + z)
                push(gains_x.at[x], gains_x.at[x], gain_send.at[2], gain_recv.at[2], device)
        else:
            wait_for(gains_x.at[0:3], gain_recv.at[2])
            gains_z[pl.ds(z, 1)] = jnp.sum(gains_x[...], axis=0, keepdims=True)
            for offset in range(1, 8):
                device = (row, x * 8 + (z + offset) % 8)
                push(gains_z.at[z], gains_z.at[z], gain_send.at[3], gain_recv.at[3], device)

    level_start(0)

    ext_t[:, 0:ROWS] = features_ref[...].T

    def spread_taps(group):
        def one_tap(tap, carry):
            index = neighbours_ref[pl.ds(tap, 1), :]
            for first in range(0, SLOTS, 256):
                places = lax.broadcasted_iota(jnp.int16, (256, ROWS), 0)
                hit = places == (index - first).astype(jnp.int16)
                chosen = jnp.where(hit, bf16(1), bf16(0))
                part = jnp.dot(chosen, grad_ref[...], preferred_element_type=f32)
                spread[tap, first : first + 256, :] = part.astype(bf16)
            return carry

        lax.fori_loop(group * T, jnp.minimum(group * T + T, TAPS), one_tap, 0)

    def weight_taps(group):
        def one_tap(tap, carry):
            wpart[pl.ds(pl.multiple_of(tap * C, C), C), :] = jnp.dot(
                ext_t[...], spread[tap], preferred_element_type=f32
            )
            return carry

        lax.fori_loop(group * T, jnp.minimum(group * T + T, TAPS), one_tap, 0)

    def prologue(group, carry):
        spread_taps(group)

        @pl.when(group == 0)
        def _():
            wait_for(wanted.at[0 : PEERS - 1], halo_recv.at[0])
            lists = jnp.broadcast_to(wanted[...], (PEERS, BUCKET, 128)).reshape(GHOSTS, 128)
            lanes = lax.broadcasted_iota(jnp.int32, (GHOSTS, 128), 1)
            places = lax.broadcasted_iota(jnp.int32, (GHOSTS, 128), 0) % BUCKET
            picked = jnp.where(lanes == places, lists.astype(f32), 0.0)
            octant = jnp.sum(picked, axis=1, keepdims=True).astype(jnp.int32)
            octants = lax.broadcasted_iota(jnp.int32, (GHOSTS, ROWS), 1)
            chosen = jnp.where(octants == octant, 1.0, 0.0).astype(bf16)
            outgoing[...] = jnp.dot(chosen, features_ref[...], preferred_element_type=f32).astype(
                bf16
            )

            def give(offset, carry):
                peer = (col + offset) % PEERS
                there = pl.ds(pl.multiple_of(peer * BUCKET, BUCKET), BUCKET)
                push(
                    outgoing.at[there],
                    ghosts.at[own],
                    halo_send.at[1],
                    halo_recv.at[1],
                    (row, peer),
                )
                return carry

            lax.fori_loop(1, PEERS, give, 0)
            owner_t[...] = chosen.T

        return carry

    lax.fori_loop(0, AHEAD, prologue, 0)
    wait_for(ghosts.at[0 : GHOSTS - BUCKET], halo_recv.at[1])
    ext_t[:, ROWS:] = ghosts[...].T

    def first_of(group):
        odd = group % 2
        return odd, y + (x - y) * odd, x + (y - x) * odd

    def peer_first(odd, other):
        return ((other + (y - other) * odd) * 2 + core, (x + (other - x) * odd) * 8 + z)

    def peer_second(odd, other):
        return ((y + (other - y) * odd) * 2 + core, (other + (x - other) * odd) * 8 + z)

    other_core = (y * 2 + 1 - core, col)

    def rows_of(start, size):
        return pl.ds(pl.multiple_of(start, PIECE), size)

    def stage0(group):
        weight_taps(group)
        base = group * R
        push(
            wpart.at[rows_of(base + (1 - core) * HALF, HALF)],
            r0.at[group],
            send.at[0, group],
            recv.at[0, group],
            other_core,
        )

    def stage1(group):
        odd, first, second = first_of(group)
        wait_for(r0.at[group], recv.at[0, group])
        mine = rows_of(group * R + core * HALF, HALF)
        a1[group] = (wpart[mine, :] + r0[group]).astype(bf16)
        for offset in range(1, 4):
            other = (first + offset) % 4
            push(
                a1.at[group, rows_of(other * QUARTER, QUARTER)],
                r1.at[group, offset - 1],
                send.at[1, group],
                recv.at[1, group],
                peer_first(odd, other),
            )

    def stage2(group):
        odd, first, second = first_of(group)
        wait_for(r1.at[group], recv.at[1, group])
        mine = rows_of(group * R + core * HALF + first * QUARTER, QUARTER)
        kept = wpart[mine, :] + r0[group, rows_of(first * QUARTER, QUARTER), :]
        for offset in range(3):
            kept = kept + r1[group, offset].astype(f32)
        a2[group] = kept.astype(bf16)
        for offset in range(1, 4):
            other = (second + offset) % 4
            push(
                a2.at[group, rows_of(other * PIECE, PIECE)],
                r2.at[group, offset - 1],
                send.at[2, group],
                recv.at[2, group],
                peer_second(odd, other),
            )

    def stage3(group):
        odd, first, second = first_of(group)
        wait_for(r2.at[group], recv.at[2, group])
        kept = a2[group, rows_of(second * PIECE, PIECE), :].astype(f32)
        for offset in range(3):
            kept = kept + r2[group, offset].astype(f32)
        r3[group, pl.ds(z, 1)] = kept.astype(bf16)[None]
        for offset in range(1, 8):
            push(
                r3.at[group, z],
                r3.at[group, z],
                send.at[3, group],
                recv.at[3, group],
                (row, x * 8 + (z + offset) % 8),
            )

    def stage4(group):
        odd, first, second = first_of(group)
        wait_for(r3.at[group, 0:7], recv.at[3, group])
        kept = r3[group, 0].astype(f32)
        for place in range(1, 8):
            kept = kept + r3[group, place].astype(f32)
        mine = rows_of(group * R + core * HALF + first * QUARTER + second * PIECE, PIECE)
        wsum_ref[mine, :] = kept.astype(bf16)
        for offset in range(1, 4):
            other = (second + offset) % 4
            push(
                wsum_ref.at[mine],
                wsum_ref.at[mine],
                send.at[4, group],
                recv.at[4, group],
                peer_second(odd, other),
            )

    def stage5(group):
        odd, first, second = first_of(group)
        wait_for(r2.at[group], recv.at[4, group])
        mine = rows_of(group * R + core * HALF + first * QUARTER, QUARTER)
        for offset in range(1, 4):
            other = (first + offset) % 4
            push(
                wsum_ref.at[mine],
                wsum_ref.at[mine],
                send.at[5, group],
                recv.at[5, group],
                peer_first(odd, other),
            )

    def stage6(group):
        wait_for(r1.at[group], recv.at[5, group])
        mine = rows_of(group * R + core * HALF, HALF)
        push(
            wsum_ref.at[mine],
            wsum_ref.at[mine],
            send.at[6, group],
            recv.at[6, group],
            other_core,
        )

    def stage7(group):
        wait_for(a1.at[group], recv.at[6, group])

        def chunk(part, carry):
            value = wsum_ref[rows_of(group * R + part * 64, 64), :].astype(f32)
            squares[...] += jnp.sum((value * value).reshape(8, 8, C), axis=0)
            return carry

        lax.fori_loop(0, R // 64, chunk, 0)

    stages = (stage0, stage1, stage2, stage3, stage4, stage5, stage6, stage7)

    def conv_tap(tap, start, size):
        total[start : start + size, :] += lax.dot_general(
            spread[tap, start : start + size, :],
            weight[tap],
            (((1,), (1,)), ((), ())),
            preferred_element_type=f32,
        )

    def step(now, carry):
        for late, stage in enumerate(stages):
            group = now - late

            @pl.when(jnp.logical_and(group >= 0, group < NG))
            def _(stage=stage, group=group):
                stage(group)

        for level in range(LEV):

            @pl.when(now == level)
            def _(level=level):
                level_end(level)

        for stage in range(1, 4):

            @pl.when(now == LEV - 1 + stage)
            def _(stage=stage):
                gain_stage(stage)

        @pl.when(now < LAST_H)
        def _():
            spread_taps(now + AHEAD)

        @pl.when(now == LAST_H)
        def _():
            weight_copy.wait()

            def ghost_tap(tap, carry):
                conv_tap(tap, ROWS, GHOSTS)
                return carry

            lax.fori_loop(0, TAPS, ghost_tap, 0)
            terms[...] = total[ROWS:, :].astype(bf16)

            def give_back(offset, carry):
                peer = (col + offset) % PEERS
                there = pl.ds(pl.multiple_of(peer * BUCKET, BUCKET), BUCKET)
                push(
                    terms.at[there],
                    returned.at[own],
                    halo_send.at[2],
                    halo_recv.at[2],
                    (row, peer),
                )
                return carry

            lax.fori_loop(1, PEERS, give_back, 0)

        @pl.when(now > LAST_H)
        def _():
            def own_tap(tap, carry):
                conv_tap(tap, 0, ROWS)
                return carry

            begin = jnp.minimum((now - LAST_H - 1) * 5, TAPS)
            lax.fori_loop(begin, jnp.minimum(begin + 5, TAPS), own_tap, 0)

        @pl.when(now == LAST_H + 7)
        def _():
            wait_for(returned.at[0 : GHOSTS - BUCKET], halo_recv.at[2])
            term = pooled[...] * gainf[...]
            high = term.astype(bf16)
            rest = term - high.astype(f32)
            middle = rest.astype(bf16)
            low = (rest - middle.astype(f32)).astype(bf16)
            mask_rows = maskf[...]
            masks = jnp.concatenate([mask_rows, mask_rows, mask_rows], axis=0).T.astype(bf16)
            parts = jnp.concatenate([high.astype(f32), middle.astype(f32), low.astype(f32)], axis=0)
            for first in range(0, ROWS, 256):
                block = slice(first, first + 256)
                value = total[block, :] + jnp.dot(
                    owner_t[block, :], returned[...], preferred_element_type=f32
                )
                value = value + jnp.dot(
                    masks[block, :], parts.astype(bf16), preferred_element_type=f32
                )
                fgrad_ref[block, :] = value.astype(bf16)

        return carry

    lax.fori_loop(0, STEPS, step, 0)

    wait_for(gains_z.at[0:7], gain_recv.at[3])
    gain_total = gains_z[0]
    for place in range(1, 8):
        gain_total = gain_total + gains_z[place]
    both = squares[...] + gain_total * gain_total
    norm2 = jnp.sum(jnp.sum(both, axis=1, keepdims=True), axis=0, keepdims=True) + tiny_eps
    factor = jnp.minimum(1.0, clip_norm / jnp.sqrt(norm2))
    gain_out[...] = gain_total * factor
    scale_out[...] = jnp.broadcast_to(factor, (8, 128))

    def finish(group, carry):
        wait_for(r0.at[group], send.at[0, group])
        wait_for(r1.at[group], send.at[1, group])
        wait_for(r2.at[group], send.at[2, group])
        wait_for(r3.at[group, 0:7], send.at[3, group])
        wait_for(r2.at[group], send.at[4, group])
        wait_for(r1.at[group], send.at[5, group])
        wait_for(a1.at[group], send.at[6, group])
        return carry

    lax.fori_loop(0, NG, finish, 0)
    wait_for(wanted.at[0 : PEERS - 1], halo_send.at[0])
    wait_for(ghosts.at[0 : GHOSTS - BUCKET], halo_send.at[1])
    wait_for(ghosts.at[0 : GHOSTS - BUCKET], halo_send.at[2])
    for level in range(LEV):
        wait_for(level_in.at[level], level_send.at[level])
    wait_for(gains0.at[0], gain_send.at[0])
    wait_for(gains_y.at[0:3], gain_send.at[1])
    wait_for(gains_x.at[0:3], gain_send.at[2])
    wait_for(gains_z.at[0:7], gain_send.at[3])


def on_device(features, grad_out, conv_weight, pool_gain, neighbours, requests, pool_mask):
    lists = jnp.pad(requests, ((0, 0), (0, 128 - BUCKET)))[:, None, :]
    vmem = pl.BlockSpec(memory_space=pltpu.VMEM)
    dma = pltpu.SemaphoreType.DMA
    feature_grad, weight_sum, gain_grad, scale = pl.pallas_call(
        whole,
        out_shape=(
            jax.ShapeDtypeStruct((ROWS, C), bf16),
            jax.ShapeDtypeStruct((NG * R, C), bf16),
            jax.ShapeDtypeStruct((8, C), f32),
            jax.ShapeDtypeStruct((8, 128), f32),
        ),
        in_specs=[vmem] * 6 + [pl.BlockSpec(memory_space=pl.ANY)],
        out_specs=(vmem, vmem, vmem, vmem),
        scratch_shapes=[
            pltpu.VMEM((TAPS, SLOTS, C), bf16),
            pltpu.VMEM((C, SLOTS), bf16),
            pltpu.VMEM((NG * R, C), f32),
            pltpu.VMEM((NG, HALF, C), f32),
            pltpu.VMEM((NG, HALF, C), bf16),
            pltpu.VMEM((NG, 3, QUARTER, C), bf16),
            pltpu.VMEM((NG, QUARTER, C), bf16),
            pltpu.VMEM((NG, 3, PIECE, C), bf16),
            pltpu.VMEM((NG, 8, PIECE, C), bf16),
            pltpu.VMEM((TAPS, C, C), bf16),
            pltpu.VMEM((SLOTS, C), f32),
            pltpu.VMEM((PEERS, 1, 128), jnp.int32),
            pltpu.VMEM((ROWS, GHOSTS), bf16),
            pltpu.VMEM((GHOSTS, C), bf16),
            pltpu.VMEM((GHOSTS, C), bf16),
            pltpu.VMEM((GHOSTS, C), bf16),
            pltpu.VMEM((GHOSTS, C), bf16),
            pltpu.VMEM((8, ROWS), f32),
            pltpu.VMEM((8, C), f32),
            pltpu.VMEM((LEV, 8, C), f32),
            pltpu.VMEM((LEV, 8, C), f32),
            pltpu.VMEM((8, C), f32),
            pltpu.VMEM((2, 8, C), f32),
            pltpu.VMEM((4, 8, C), f32),
            pltpu.VMEM((4, 8, C), f32),
            pltpu.VMEM((8, 8, C), f32),
            pltpu.VMEM((8, C), f32),
            dma((7, NG)),
            dma((7, NG)),
            dma((3,)),
            dma((3,)),
            dma((LEV,)),
            dma((LEV,)),
            dma((4,)),
            dma((4,)),
            dma,
        ],
        compiler_params=pltpu.CompilerParams(
            collective_id=0, has_side_effects=True, vmem_limit_bytes=58 * 2**20
        ),
    )(features, grad_out, neighbours, lists, pool_mask, pool_gain, conv_weight)
    weight_sum = weight_sum[: TAPS * C].reshape(TAPS, C, C)
    return (feature_grad, weight_sum.astype(f32) * scale[0, 0], gain_grad[:LEV])


def solution(mesh):
    placed = (
        P(("row", "col"), None),
        P(("row", "col"), None),
        P(),
        P(),
        P(None, ("row", "col")),
        P(("row", "col"), None),
        P(None, ("row", "col")),
    )
    return jax.shard_map(
        on_device,
        mesh=mesh,
        in_specs=placed,
        out_specs=(P(("row", "col"), None), P(), P()),
        check_vma=False,
    )
```

```python
import jax
import jax.numpy as jnp
from jax import lax
from jax.experimental import pallas as pl
from jax.experimental.pallas import tpu as pltpu
from jax.sharding import PartitionSpec as P

MESH = pl.DeviceIdType.MESH
clip_norm = 1024.0
tiny_eps = 1e-06
ROWS = 1024
C = 256
TAPS = 27
BUCKET = 16
PEERS = 32
GHOSTS = PEERS * BUCKET
SLOTS = ROWS + GHOSTS
LEV = 5
T = 2
NG = 28 // T
R = T * C
HALF = R // 2
QUARTER = HALF // 4
PIECE = HALF // 16
READY = 8 // T
STEPS = NG + 7
f32 = jnp.float32
bf16 = jnp.bfloat16


def wait_for(ref, sem):
    pltpu.make_async_copy(ref, ref, sem).wait()


def whole(
    features_ref,
    grad_ref,
    neighbours_ref,
    requests_ref,
    mask_ref,
    gain_ref,
    weight_hbm,
    fgrad_ref,
    wsum_ref,
    gain_out,
    scale_out,
    spread,
    ext_t,
    wpart,
    r0,
    a1,
    r1,
    a2,
    r2,
    r3,
    weight,
    total,
    asked,
    wanted,
    owner_t,
    outgoing,
    ghosts,
    terms,
    returned,
    maskf,
    gainf,
    level_out,
    level_in,
    pooled,
    gains0,
    gains_y,
    gains_x,
    gains_z,
    squares,
    send,
    recv,
    halo_send,
    halo_recv,
    level_send,
    level_recv,
    gain_send,
    gain_recv,
    weight_sem,
):
    row = lax.axis_index("row")
    col = lax.axis_index("col")
    y = row // 2
    core = row % 2
    x = col // 8
    z = col % 8

    def push(src, dst, send_sem, recv_sem, device):
        pltpu.make_async_remote_copy(
            src_ref=src,
            dst_ref=dst,
            send_sem=send_sem,
            recv_sem=recv_sem,
            device_id=device,
            device_id_type=MESH,
        ).start()

    weight_copy = pltpu.make_async_copy(weight_hbm, weight, weight_sem)
    weight_copy.start()

    barrier = pltpu.get_barrier_semaphore()

    def greet(offset, carry):
        pl.semaphore_signal(
            barrier, inc=1, device_id=(row, (col + offset) % PEERS), device_id_type=MESH
        )
        return carry

    lax.fori_loop(1, PEERS, greet, 0)
    pl.semaphore_signal(barrier, inc=1, device_id=(y * 2 + 1 - core, col), device_id_type=MESH)
    for offset in range(1, 4):
        pl.semaphore_signal(
            barrier, inc=1, device_id=((y + offset) % 4 * 2 + core, col), device_id_type=MESH
        )

    maskf[...] = jnp.zeros_like(maskf)
    maskf[0:LEV, :] = mask_ref[...].astype(f32)
    gainf[...] = jnp.zeros_like(gainf)
    gainf[0:LEV, :] = gain_ref[...]
    level_out[0] = jnp.dot(maskf[...].astype(bf16), grad_ref[...], preferred_element_type=f32)
    square = jnp.concatenate([requests_ref[...], jnp.zeros((128 - BUCKET, PEERS), jnp.int32)], axis=0)
    lists = square.astype(f32).T.astype(jnp.int32)
    for peer in range(PEERS):
        asked[peer] = lists[peer : peer + 1, :]
    wanted[pl.ds(col, 1)] = jnp.zeros((1, 1, 128), jnp.int32)
    own = pl.ds(pl.multiple_of(col * BUCKET, BUCKET), BUCKET)
    ghosts[own, :] = jnp.zeros((BUCKET, C), bf16)
    returned[own, :] = jnp.zeros((BUCKET, C), bf16)
    wpart[TAPS * C :, :] = jnp.zeros(((NG * T - TAPS) * C, C), f32)
    squares[...] = jnp.zeros_like(squares)
    total[...] = jnp.zeros_like(total)
    ext_t[:, 0:ROWS] = features_ref[...].T

    pl.semaphore_wait(barrier, PEERS - 1 + 1 + 3)

    def ask(offset, carry):
        peer = (col + offset) % PEERS
        push(asked.at[peer], wanted.at[col], halo_send.at[0], halo_recv.at[0], (row, peer))
        return carry

    lax.fori_loop(1, PEERS, ask, 0)

    level_partner = (
        ((y + 2) % 4 * 2 + core, col),
        ((y + 1 - 2 * (y % 2)) * 2 + core, col),
        (y * 2 + 1 - core, col),
        (row, (x + 2) % 4 * 8 + z),
        (row, (x + 1 - 2 * (x % 2)) * 8 + z),
    )

    def level_start(level):
        push(
            level_out.at[level],
            level_in.at[level],
            level_send.at[level],
            level_recv.at[level],
            level_partner[level],
        )

    level_rows = lax.broadcasted_iota(jnp.int32, (8, C), 0)

    def level_end(level):
        wait_for(level_in.at[level], level_recv.at[level])
        summed = level_out[level] + jnp.where(level_rows >= level, level_in[level], 0.0)
        if level < LEV - 1:
            level_out[level + 1] = summed
            level_start(level + 1)
            return
        scale = jnp.zeros((8, C), f32)
        for row_level in range(LEV):
            value = (2.0 ** (row_level + 1) * ROWS) ** (-0.5)
            scale = jnp.where(level_rows == row_level, value, scale)
        pooled[...] = summed * scale
        feature_sums = jnp.dot(
            maskf[...].astype(bf16), features_ref[...], preferred_element_type=f32
        )
        gains0[0] = feature_sums * pooled[...]
        push(
            gains0.at[0], gains0.at[1], gain_send.at[0], gain_recv.at[0], (y * 2 + 1 - core, col)
        )

    def gain_stage(stage):
        if stage == 1:
            wait_for(gains0.at[1], gain_recv.at[0])
            gains_y[pl.ds(y, 1)] = (gains0[0] + gains0[1])[None]
            for offset in range(1, 4):
                device = ((y + offset) % 4 * 2 + core, col)
                push(gains_y.at[y], gains_y.at[y], gain_send.at[1], gain_recv.at[1], device)
        elif stage == 2:
            wait_for(gains_y.at[0:3], gain_recv.at[1])
            gains_x[pl.ds(x, 1)] = jnp.sum(gains_y[...], axis=0, keepdims=True)
            for offset in range(1, 4):
                device = (row, (x + offset) % 4 * 8 + z)
                push(gains_x.at[x], gains_x.at[x], gain_send.at[2], gain_recv.at[2], device)
        else:
            wait_for(gains_x.at[0:3], gain_recv.at[2])
            gains_z[pl.ds(z, 1)] = jnp.sum(gains_x[...], axis=0, keepdims=True)
            for offset in range(1, 8):
                device = (row, x * 8 + (z + offset) % 8)
                push(gains_z.at[z], gains_z.at[z], gain_send.at[3], gain_recv.at[3], device)

    level_start(0)

    def each_pair(group, body):
        def pair(number, carry):
            body(number * 2, 2)
            return carry

        lax.fori_loop(group * (T // 2), jnp.minimum((group + 1) * (T // 2), TAPS // 2), pair, 0)

        @pl.when(group == NG - 1)
        def _():
            body(TAPS - 1, 1)

    def spread_taps(group):
        def body(begin, count):
            for late in range(count):
                index = neighbours_ref[pl.ds(begin + late, 1), :]
                for first in range(0, SLOTS, 256):
                    places = lax.broadcasted_iota(jnp.int16, (256, ROWS), 0)
                    hit = places == (index - first).astype(jnp.int16)
                    chosen = jnp.where(hit, bf16(1), bf16(0))
                    part = jnp.dot(chosen, grad_ref[...], preferred_element_type=f32)
                    spread[begin + late, first : first + 256, :] = part.astype(bf16)

        each_pair(group, body)

    def weight_taps(group):
        def body(begin, count):
            for late in range(count):
                tap = begin + late
                wpart[pl.ds(pl.multiple_of(tap * C, C), C), :] = jnp.dot(
                    ext_t[...], spread[tap], preferred_element_type=f32
                )

        each_pair(group, body)

    def give_features():
        wait_for(wanted.at[0 : PEERS - 1], halo_recv.at[0])
        lists = jnp.broadcast_to(wanted[...], (PEERS, BUCKET, 128)).reshape(GHOSTS, 128)
        lanes = lax.broadcasted_iota(jnp.int32, (GHOSTS, 128), 1)
        places = lax.broadcasted_iota(jnp.int32, (GHOSTS, 128), 0) % BUCKET
        picked = jnp.where(lanes == places, lists.astype(f32), 0.0)
        octant = jnp.sum(picked, axis=1, keepdims=True).astype(jnp.int32)
        octants = lax.broadcasted_iota(jnp.int32, (GHOSTS, ROWS), 1)
        chosen = jnp.where(octants == octant, 1.0, 0.0).astype(bf16)
        outgoing[...] = jnp.dot(chosen, features_ref[...], preferred_element_type=f32).astype(bf16)

        def give(offset, carry):
            peer = (col + offset) % PEERS
            there = pl.ds(pl.multiple_of(peer * BUCKET, BUCKET), BUCKET)
            push(outgoing.at[there], ghosts.at[own], halo_send.at[1], halo_recv.at[1], (row, peer))
            return carry

        lax.fori_loop(1, PEERS, give, 0)
        owner_t[...] = chosen.T

    def first_of(group):
        odd = (group + group // 4) % 2
        return odd, y + (x - y) * odd, x + (y - x) * odd

    def peer_first(odd, other):
        return ((other + (y - other) * odd) * 2 + core, (x + (other - x) * odd) * 8 + z)

    def peer_second(odd, other):
        return ((y + (other - y) * odd) * 2 + core, (other + (x - other) * odd) * 8 + z)

    other_core = (y * 2 + 1 - core, col)

    def rows_of(start, size):
        return pl.ds(pl.multiple_of(start, PIECE), size)

    def stage0(group):
        weight_taps(group)
        base = group * R
        push(
            wpart.at[rows_of(base + (1 - core) * HALF, HALF)],
            r0.at[group],
            send.at[0, group],
            recv.at[0, group],
            other_core,
        )

    def stage1(group):
        odd, first, second = first_of(group)
        wait_for(r0.at[group], recv.at[0, group])
        mine = rows_of(group * R + core * HALF, HALF)
        a1[group] = (wpart[mine, :] + r0[group]).astype(bf16)
        for offset in range(1, 4):
            other = (first + offset) % 4
            push(
                a1.at[group, rows_of(other * QUARTER, QUARTER)],
                r1.at[group, offset - 1],
                send.at[1, group],
                recv.at[1, group],
                peer_first(odd, other),
            )

    def stage2(group):
        odd, first, second = first_of(group)
        wait_for(r1.at[group], recv.at[1, group])
        mine = rows_of(group * R + core * HALF + first * QUARTER, QUARTER)
        kept = wpart[mine, :] + r0[group, rows_of(first * QUARTER, QUARTER), :]
        for offset in range(3):
            kept = kept + r1[group, offset].astype(f32)
        a2[group] = kept.astype(bf16)
        for offset in range(1, 4):
            other = (second + offset) % 4
            push(
                a2.at[group, rows_of(other * PIECE, PIECE)],
                r2.at[group, offset - 1],
                send.at[2, group],
                recv.at[2, group],
                peer_second(odd, other),
            )

    def stage3(group):
        odd, first, second = first_of(group)
        wait_for(r2.at[group], recv.at[2, group])
        kept = a2[group, rows_of(second * PIECE, PIECE), :].astype(f32)
        for offset in range(3):
            kept = kept + r2[group, offset].astype(f32)
        r3[group, pl.ds(z, 1)] = kept.astype(bf16)[None]
        for offset in range(1, 8):
            push(
                r3.at[group, z],
                r3.at[group, z],
                send.at[3, group],
                recv.at[3, group],
                (row, x * 8 + (z + offset) % 8),
            )

    def stage4(group):
        odd, first, second = first_of(group)
        wait_for(r3.at[group, 0:7], recv.at[3, group])
        kept = r3[group, 0].astype(f32)
        for place in range(1, 8):
            kept = kept + r3[group, place].astype(f32)
        mine = rows_of(group * R + core * HALF + first * QUARTER + second * PIECE, PIECE)
        wsum_ref[mine, :] = kept.astype(bf16)
        for offset in range(1, 4):
            other = (second + offset) % 4
            push(
                wsum_ref.at[mine],
                wsum_ref.at[mine],
                send.at[4, group],
                recv.at[4, group],
                peer_second(odd, other),
            )

    def stage5(group):
        odd, first, second = first_of(group)
        wait_for(r2.at[group], recv.at[4, group])
        mine = rows_of(group * R + core * HALF + first * QUARTER, QUARTER)
        for offset in range(1, 4):
            other = (first + offset) % 4
            push(
                wsum_ref.at[mine],
                wsum_ref.at[mine],
                send.at[5, group],
                recv.at[5, group],
                peer_first(odd, other),
            )

    def stage6(group):
        wait_for(r1.at[group], recv.at[5, group])
        mine = rows_of(group * R + core * HALF, HALF)
        push(
            wsum_ref.at[mine],
            wsum_ref.at[mine],
            send.at[6, group],
            recv.at[6, group],
            other_core,
        )

    def stage7(group):
        wait_for(a1.at[group], recv.at[6, group])

        def chunk(part, carry):
            value = wsum_ref[rows_of(group * R + part * 64, 64), :].astype(f32)
            squares[...] += jnp.sum((value * value).reshape(8, 8, C), axis=0)
            return carry

        lax.fori_loop(0, R // 64, chunk, 0)

    stages = (stage0, stage1, stage2, stage3, stage4, stage5, stage6, stage7)

    def conv_taps(begin, count, start, size):
        value = total[start : start + size, :]
        for late in range(count):
            value = value + lax.dot_general(
                spread[begin + late, start : start + size, :],
                weight[begin + late],
                (((1,), (1,)), ((), ())),
                preferred_element_type=f32,
            )
        total[start : start + size, :] = value

    def step(now, carry):
        @pl.when(now == 1)
        def _():
            give_features()

        @pl.when(now == READY)
        def _():
            wait_for(ghosts.at[0 : GHOSTS - BUCKET], halo_recv.at[1])
            ext_t[:, ROWS:] = ghosts[...].T

        @pl.when(now < NG)
        def _():
            spread_taps(now)

        for late, stage in enumerate(stages):
            made = now - late
            double = jnp.logical_and(made >= READY, made < 2 * READY).astype(jnp.int32)
            single = jnp.logical_and(made >= 2 * READY, made < NG).astype(jnp.int32)
            begin = double * 2 * (made - READY) + single * made

            def run(group, carry, stage=stage):
                stage(group)
                return carry

            lax.fori_loop(begin, begin + 2 * double + single, run, 0)

        for level in range(LEV):

            @pl.when(now == level + 1)
            def _(level=level):
                level_end(level)

        for stage in range(1, 4):

            @pl.when(now == LEV + stage)
            def _(stage=stage):
                gain_stage(stage)

        @pl.when(now == NG)
        def _():
            weight_copy.wait()

            def ghost_taps(number, carry):
                conv_taps(number * 3, 3, ROWS, GHOSTS)
                return carry

            lax.fori_loop(0, TAPS // 3, ghost_taps, 0)
            terms[...] = total[ROWS:, :].astype(bf16)

            def give_back(offset, carry):
                peer = (col + offset) % PEERS
                there = pl.ds(pl.multiple_of(peer * BUCKET, BUCKET), BUCKET)
                push(
                    terms.at[there],
                    returned.at[own],
                    halo_send.at[2],
                    halo_recv.at[2],
                    (row, peer),
                )
                return carry

            lax.fori_loop(1, PEERS, give_back, 0)

        @pl.when(now > NG)
        def _():
            def own_taps(number, carry):
                conv_taps(number * 3, 3, 0, ROWS)
                return carry

            begin = jnp.minimum((now - NG - 1) * 2, TAPS // 3)
            lax.fori_loop(begin, jnp.minimum(begin + 2, TAPS // 3), own_taps, 0)

        @pl.when(now == STEPS - 1)
        def _():
            wait_for(returned.at[0 : GHOSTS - BUCKET], halo_recv.at[2])
            term = pooled[...] * gainf[...]
            high = term.astype(bf16)
            rest = term - high.astype(f32)
            middle = rest.astype(bf16)
            low = (rest - middle.astype(f32)).astype(bf16)
            mask_rows = maskf[...]
            masks = jnp.concatenate([mask_rows, mask_rows, mask_rows], axis=0).T.astype(bf16)
            parts = jnp.concatenate([high.astype(f32), middle.astype(f32), low.astype(f32)], axis=0)
            for first in range(0, ROWS, 256):
                block = slice(first, first + 256)
                value = total[block, :] + jnp.dot(
                    owner_t[block, :], returned[...], preferred_element_type=f32
                )
                value = value + jnp.dot(
                    masks[block, :], parts.astype(bf16), preferred_element_type=f32
                )
                fgrad_ref[block, :] = value.astype(bf16)

        return carry

    lax.fori_loop(0, STEPS, step, 0)

    wait_for(gains_z.at[0:7], gain_recv.at[3])
    gain_total = gains_z[0]
    for place in range(1, 8):
        gain_total = gain_total + gains_z[place]
    both = squares[...] + gain_total * gain_total
    norm2 = jnp.sum(jnp.sum(both, axis=1, keepdims=True), axis=0, keepdims=True) + tiny_eps
    factor = jnp.minimum(1.0, clip_norm / jnp.sqrt(norm2))
    gain_out[...] = gain_total * factor
    scale_out[...] = factor

    def finish(group, carry):
        wait_for(r0.at[group], send.at[0, group])
        wait_for(r1.at[group], send.at[1, group])
        wait_for(r2.at[group], send.at[2, group])
        wait_for(r3.at[group, 0:7], send.at[3, group])
        wait_for(r2.at[group], send.at[4, group])
        wait_for(r1.at[group], send.at[5, group])
        wait_for(a1.at[group], send.at[6, group])
        return carry

    lax.fori_loop(0, NG, finish, 0)
    wait_for(wanted.at[0 : PEERS - 1], halo_send.at[0])
    wait_for(ghosts.at[0 : GHOSTS - BUCKET], halo_send.at[1])
    wait_for(ghosts.at[0 : GHOSTS - BUCKET], halo_send.at[2])
    for level in range(LEV):
        wait_for(level_in.at[level], level_send.at[level])
    wait_for(gains0.at[0], gain_send.at[0])
    wait_for(gains_y.at[0:3], gain_send.at[1])
    wait_for(gains_x.at[0:3], gain_send.at[2])
    wait_for(gains_z.at[0:7], gain_send.at[3])


def on_device(features, grad_out, conv_weight, pool_gain, neighbours, requests, pool_mask):
    vmem = pl.BlockSpec(memory_space=pltpu.VMEM)
    dma = pltpu.SemaphoreType.DMA
    feature_grad, weight_sum, gain_grad, scale = pl.pallas_call(
        whole,
        out_shape=(
            jax.ShapeDtypeStruct((ROWS, C), bf16),
            jax.ShapeDtypeStruct((NG * R, C), bf16),
            jax.ShapeDtypeStruct((8, C), f32),
            jax.ShapeDtypeStruct((1, 1), f32),
        ),
        in_specs=[vmem] * 6 + [pl.BlockSpec(memory_space=pl.ANY)],
        out_specs=(vmem, vmem, vmem, vmem),
        scratch_shapes=[
            pltpu.VMEM((TAPS, SLOTS, C), bf16),
            pltpu.VMEM((C, SLOTS), bf16),
            pltpu.VMEM((NG * R, C), f32),
            pltpu.VMEM((NG, HALF, C), f32),
            pltpu.VMEM((NG, HALF, C), bf16),
            pltpu.VMEM((NG, 3, QUARTER, C), bf16),
            pltpu.VMEM((NG, QUARTER, C), bf16),
            pltpu.VMEM((NG, 3, PIECE, C), bf16),
            pltpu.VMEM((NG, 8, PIECE, C), bf16),
            pltpu.VMEM((TAPS, C, C), bf16),
            pltpu.VMEM((SLOTS, C), f32),
            pltpu.VMEM((PEERS, 1, 128), jnp.int32),
            pltpu.VMEM((PEERS, 1, 128), jnp.int32),
            pltpu.VMEM((ROWS, GHOSTS), bf16),
            pltpu.VMEM((GHOSTS, C), bf16),
            pltpu.VMEM((GHOSTS, C), bf16),
            pltpu.VMEM((GHOSTS, C), bf16),
            pltpu.VMEM((GHOSTS, C), bf16),
            pltpu.VMEM((8, ROWS), f32),
            pltpu.VMEM((8, C), f32),
            pltpu.VMEM((LEV, 8, C), f32),
            pltpu.VMEM((LEV, 8, C), f32),
            pltpu.VMEM((8, C), f32),
            pltpu.VMEM((2, 8, C), f32),
            pltpu.VMEM((4, 8, C), f32),
            pltpu.VMEM((4, 8, C), f32),
            pltpu.VMEM((8, 8, C), f32),
            pltpu.VMEM((8, C), f32),
            dma((7, NG)),
            dma((7, NG)),
            dma((3,)),
            dma((3,)),
            dma((LEV,)),
            dma((LEV,)),
            dma((4,)),
            dma((4,)),
            dma,
        ],
        compiler_params=pltpu.CompilerParams(
            collective_id=0, has_side_effects=True, vmem_limit_bytes=58 * 2**20
        ),
    )(features, grad_out, neighbours, requests.T, pool_mask, pool_gain, conv_weight)
    weight_sum = weight_sum[: TAPS * C].reshape(TAPS, C, C)
    return (feature_grad, weight_sum.astype(f32) * scale[0, 0], gain_grad[:LEV])


def solution(mesh):
    placed = (
        P(("row", "col"), None),
        P(("row", "col"), None),
        P(),
        P(),
        P(None, ("row", "col")),
        P(("row", "col"), None),
        P(None, ("row", "col")),
    )
    return jax.shard_map(
        on_device,
        mesh=mesh,
        in_specs=placed,
        out_specs=(P(("row", "col"), None), P(), P()),
        check_vma=False,
    )
```

```python
import jax
import jax.numpy as jnp
from jax import lax
from jax.experimental import pallas as pl
from jax.experimental.pallas import tpu as pltpu
from jax.sharding import PartitionSpec as P

MESH = pl.DeviceIdType.MESH
clip_norm = 1024.0
tiny_eps = 1e-06
ROWS = 1024
C = 256
TAPS = 27
BUCKET = 16
PEERS = 32
GHOSTS = PEERS * BUCKET
SLOTS = ROWS + GHOSTS
LEV = 5
T = 4
NG = 28 // T
R = T * C
HALF = R // 2
QUARTER = HALF // 4
PIECE = HALF // 16
READY = 3
STEPS = NG + 7
f32 = jnp.float32
bf16 = jnp.bfloat16


def wait_for(ref, sem):
    pltpu.make_async_copy(ref, ref, sem).wait()


def whole(
    features_ref,
    grad_ref,
    neighbours_ref,
    requests_ref,
    mask_ref,
    gain_ref,
    weight_hbm,
    fgrad_ref,
    wsum_hbm,
    gain_out,
    scale_out,
    wsum_ref,
    spread,
    ext_t,
    wpart,
    r0,
    a1,
    r1,
    a2,
    r2,
    r3,
    weight,
    total,
    asked,
    asked_mid,
    wanted,
    owner_t,
    outgoing,
    outgoing_mid,
    ghosts,
    terms,
    terms_mid,
    returned,
    maskf,
    gainf,
    level_out,
    level_in,
    pooled,
    gains0,
    gains_y,
    gains_x,
    gains_z,
    squares,
    send,
    recv,
    halo_send,
    halo_recv,
    level_send,
    level_recv,
    gain_send,
    gain_recv,
    weight_sem,
    store_sem,
):
    row = lax.axis_index("row")
    col = lax.axis_index("col")
    y = row // 2
    core = row % 2
    x = col // 8
    z = col % 8
    y_others = [(y + offset) % 4 for offset in range(1, 4)]
    x_others = [(x + offset) % 4 for offset in range(1, 4)]
    z_others = [(z + offset) % 8 for offset in range(1, 8)]
    y_rows = [other * 2 + core for other in y_others]
    x_cols = [other * 8 + z for other in x_others]
    z_cols = [x * 8 + other for other in z_others]
    other_core = (y * 2 + 1 - core, col)
    y_peers = [(there, col) for there in y_rows]
    x_peers = [(row, there) for there in x_cols]
    z_peers = [(row, there) for there in z_cols]
    near = y_peers + x_peers + z_peers + [other_core]

    def push(src, dst, send_sem, recv_sem, device):
        pltpu.make_async_remote_copy(
            src_ref=src,
            dst_ref=dst,
            send_sem=send_sem,
            recv_sem=recv_sem,
            device_id=device,
            device_id_type=MESH,
        ).start()

    weight_copy = pltpu.make_async_copy(weight_hbm, weight, weight_sem)
    weight_copy.start()

    barrier = pltpu.get_barrier_semaphore()
    for device in near:
        pl.semaphore_signal(barrier, inc=1, device_id=device, device_id_type=MESH)

    maskf[...] = jnp.zeros_like(maskf)
    maskf[0:LEV, :] = mask_ref[...].astype(f32)
    gainf[...] = jnp.zeros_like(gainf)
    gainf[0:LEV, :] = gain_ref[...]
    level_out[0] = jnp.dot(maskf[...].astype(bf16), grad_ref[...], preferred_element_type=f32)
    square = jnp.concatenate([requests_ref[...], jnp.zeros((128 - BUCKET, PEERS), jnp.int32)], axis=0)
    lists = square.astype(f32).T.astype(jnp.int32)
    for peer in range(PEERS):
        asked[peer // 8, peer % 8] = lists[peer : peer + 1, :]
    wpart[TAPS * C :, :] = jnp.zeros(((NG * T - TAPS) * C, C), f32)
    squares[...] = jnp.zeros_like(squares)
    total[...] = jnp.zeros_like(total)
    ext_t[:, 0:ROWS] = features_ref[...].T

    pl.semaphore_wait(barrier, len(near))

    def leg_x(number, src, mid):
        for other, device in zip(x_others, x_peers):
            push(src.at[other], mid.at[x], halo_send.at[number], halo_recv.at[number], device)
        mid[pl.ds(x, 1)] = src[pl.ds(x, 1)]

    def leg_z(number, mid, dst):
        wait_for(mid.at[0:3], halo_recv.at[number])
        for other, device in zip(z_others, z_peers):
            push(
                mid.at[:, other],
                dst.at[:, z],
                halo_send.at[number + 1],
                halo_recv.at[number + 1],
                device,
            )
        dst[:, pl.ds(z, 1)] = mid[:, pl.ds(z, 1)]

    def leg_end(number, dst):
        wait_for(dst.at[:, 0:7], halo_recv.at[number + 1])

    leg_x(0, asked, asked_mid)

    level_partner = (
        ((y + 2) % 4 * 2 + core, col),
        ((y + 1 - 2 * (y % 2)) * 2 + core, col),
        (y * 2 + 1 - core, col),
        (row, (x + 2) % 4 * 8 + z),
        (row, (x + 1 - 2 * (x % 2)) * 8 + z),
    )

    def level_start(level):
        push(
            level_out.at[level],
            level_in.at[level],
            level_send.at[level],
            level_recv.at[level],
            level_partner[level],
        )

    level_rows = lax.broadcasted_iota(jnp.int32, (8, C), 0)

    def level_end(level):
        wait_for(level_in.at[level], level_recv.at[level])
        summed = level_out[level] + jnp.where(level_rows >= level, level_in[level], 0.0)
        if level < LEV - 1:
            level_out[level + 1] = summed
            level_start(level + 1)
            return
        scale = jnp.zeros((8, C), f32)
        for row_level in range(LEV):
            value = (2.0 ** (row_level + 1) * ROWS) ** (-0.5)
            scale = jnp.where(level_rows == row_level, value, scale)
        pooled[...] = summed * scale
        feature_sums = jnp.dot(
            maskf[...].astype(bf16), features_ref[...], preferred_element_type=f32
        )
        gains0[0] = feature_sums * pooled[...]
        push(
            gains0.at[0], gains0.at[1], gain_send.at[0], gain_recv.at[0], other_core
        )

    def gain_stage(stage):
        if stage == 1:
            wait_for(gains0.at[1], gain_recv.at[0])
            gains_y[pl.ds(y, 1)] = (gains0[0] + gains0[1])[None]
            for device in y_peers:
                push(gains_y.at[y], gains_y.at[y], gain_send.at[1], gain_recv.at[1], device)
        elif stage == 2:
            wait_for(gains_y.at[0:3], gain_recv.at[1])
            gains_x[pl.ds(x, 1)] = jnp.sum(gains_y[...], axis=0, keepdims=True)
            for device in x_peers:
                push(gains_x.at[x], gains_x.at[x], gain_send.at[2], gain_recv.at[2], device)
        else:
            wait_for(gains_x.at[0:3], gain_recv.at[2])
            gains_z[pl.ds(z, 1)] = jnp.sum(gains_x[...], axis=0, keepdims=True)
            for device in z_peers:
                push(gains_z.at[z], gains_z.at[z], gain_send.at[3], gain_recv.at[3], device)

    level_start(0)

    def each_pair(group, body):
        def pair(number, carry):
            body(number * 2, 2)
            return carry

        lax.fori_loop(group * (T // 2), jnp.minimum((group + 1) * (T // 2), TAPS // 2), pair, 0)

        @pl.when(group == NG - 1)
        def _():
            body(TAPS - 1, 1)

    def spread_pair(pair):
        def body(begin, count):
            for late in range(count):
                index = neighbours_ref[pl.ds(begin + late, 1), :]
                for first in range(0, SLOTS, 256):
                    places = lax.broadcasted_iota(jnp.int16, (256, ROWS), 0)
                    hit = places == (index - first).astype(jnp.int16)
                    chosen = jnp.where(hit, bf16(1), bf16(0))
                    part = jnp.dot(chosen, grad_ref[...], preferred_element_type=f32)
                    spread[begin + late, first : first + 256, :] = part.astype(bf16)

        @pl.when(pair < TAPS // 2)
        def _():
            body(pair * 2, 2)

        @pl.when(pair == TAPS // 2)
        def _():
            body(TAPS - 1, 1)

    def weight_taps(group):
        def body(begin, count):
            for late in range(count):
                tap = begin + late
                wpart[pl.ds(pl.multiple_of(tap * C, C), C), :] = jnp.dot(
                    ext_t[...], spread[tap], preferred_element_type=f32
                )

        each_pair(group, body)

    def give_features():
        leg_end(0, wanted)
        lists = jnp.broadcast_to(wanted[...].reshape(PEERS, 1, 128), (PEERS, BUCKET, 128)).reshape(GHOSTS, 128)
        lanes = lax.broadcasted_iota(jnp.int32, (GHOSTS, 128), 1)
        places = lax.broadcasted_iota(jnp.int32, (GHOSTS, 128), 0) % BUCKET
        picked = jnp.where(lanes == places, lists.astype(f32), 0.0)
        octant = jnp.sum(picked, axis=1, keepdims=True).astype(jnp.int32)
        octants = lax.broadcasted_iota(jnp.int32, (GHOSTS, ROWS), 1)
        chosen = jnp.where(octants == octant, 1.0, 0.0).astype(bf16)
        taken = jnp.dot(chosen, features_ref[...], preferred_element_type=f32).astype(bf16)
        outgoing[...] = taken.reshape(4, 8, BUCKET, C)
        leg_x(2, outgoing, outgoing_mid)
        owner_t[...] = chosen.T

    def order_of(group):
        odd = (group + group // 4) % 2
        return odd, y + (x - y) * odd, x + (y - x) * odd

    def peers_of(odd):
        chips = [b_ + (a_ - b_) * odd for a_, b_ in zip(x_others, y_others)]
        rows = [there + (row - there) * odd for there in y_rows]
        cols = [col + (there - col) * odd for there in x_cols]
        return zip(chips, zip(rows, cols))

    def rows_of(start, size):
        return pl.ds(pl.multiple_of(start, PIECE), size)

    def stage0(group):
        weight_taps(group)
        base = group * R
        push(
            wpart.at[rows_of(base + (1 - core) * HALF, HALF)],
            r0.at[group],
            send.at[0],
            recv.at[0, group],
            other_core,
        )

    def stage1(group):
        odd, first, second = order_of(group)
        wait_for(r0.at[group], recv.at[0, group])
        mine = rows_of(group * R + core * HALF, HALF)
        a1[group] = (wpart[mine, :] + r0[group]).astype(bf16)
        for place, (other, device) in enumerate(peers_of(odd)):
            push(
                a1.at[group, rows_of(other * QUARTER, QUARTER)],
                r1.at[group, place],
                send.at[1],
                recv.at[1, group],
                device,
            )

    def stage2(group):
        odd, first, second = order_of(group)
        wait_for(r1.at[group], recv.at[1, group])
        mine = rows_of(group * R + core * HALF + first * QUARTER, QUARTER)
        kept = wpart[mine, :] + r0[group, rows_of(first * QUARTER, QUARTER), :]
        for offset in range(3):
            kept = kept + r1[group, offset].astype(f32)
        a2[group] = kept.astype(bf16)
        for place, (other, device) in enumerate(peers_of(1 - odd)):
            push(
                a2.at[group, rows_of(other * PIECE, PIECE)],
                r2.at[group, place],
                send.at[2],
                recv.at[2, group],
                device,
            )

    def stage3(group):
        odd, first, second = order_of(group)
        wait_for(r2.at[group], recv.at[2, group])
        kept = a2[group, rows_of(second * PIECE, PIECE), :].astype(f32)
        for offset in range(3):
            kept = kept + r2[group, offset].astype(f32)
        r3[group, pl.ds(z, 1)] = kept.astype(bf16)[None]
        for device in z_peers:
            push(
                r3.at[group, z],
                r3.at[group, z],
                send.at[3],
                recv.at[3, group],
                device,
            )

    def stage4(group):
        odd, first, second = order_of(group)
        wait_for(r3.at[group, 0:7], recv.at[3, group])
        kept = r3[group, 0].astype(f32)
        for place in range(1, 8):
            kept = kept + r3[group, place].astype(f32)
        mine = rows_of(group * R + core * HALF + first * QUARTER + second * PIECE, PIECE)
        wsum_ref[mine, :] = kept.astype(bf16)
        for place, (other, device) in enumerate(peers_of(1 - odd)):
            push(
                wsum_ref.at[mine],
                wsum_ref.at[mine],
                send.at[4],
                recv.at[4, group],
                device,
            )

    def stage5(group):
        odd, first, second = order_of(group)
        wait_for(r2.at[group], recv.at[4, group])
        mine = rows_of(group * R + core * HALF + first * QUARTER, QUARTER)
        for place, (other, device) in enumerate(peers_of(odd)):
            push(
                wsum_ref.at[mine],
                wsum_ref.at[mine],
                send.at[5],
                recv.at[5, group],
                device,
            )

    def stage6(group):
        wait_for(r1.at[group], recv.at[5, group])
        mine = rows_of(group * R + core * HALF, HALF)
        push(
            wsum_ref.at[mine],
            wsum_ref.at[mine],
            send.at[6],
            recv.at[6, group],
            other_core,
        )

    def stage7(group):
        wait_for(a1.at[group], recv.at[6, group])

        def chunk(part, carry):
            value = wsum_ref[rows_of(group * R + part * 64, 64), :].astype(f32)
            squares[...] += jnp.sum((value * value).reshape(8, 8, C), axis=0)
            return carry

        done = rows_of(group * R, R)
        pltpu.make_async_copy(wsum_ref.at[done], wsum_hbm.at[done], store_sem).start()
        lax.fori_loop(0, R // 64, chunk, 0)

    stages = (stage0, stage1, stage2, stage3, stage4, stage5, stage6, stage7)

    def conv_taps(begin, count, start, size):
        value = total[start : start + size, :]
        for late in range(count):
            value = value + lax.dot_general(
                spread[begin + late, start : start + size, :],
                weight[begin + late],
                (((1,), (1,)), ((), ())),
                preferred_element_type=f32,
            )
        total[start : start + size, :] = value

    def step(now, carry):
        @pl.when(now == 1)
        def _():
            give_features()

        @pl.when(now == 2)
        def _():
            leg_z(2, outgoing_mid, ghosts)

        @pl.when(now == READY)
        def _():
            leg_end(2, ghosts)
            ext_t[:, ROWS:] = ghosts[...].reshape(GHOSTS, C).T

        @pl.when(now < NG)
        def _():
            spread_pair(now * 2)

        @pl.when(now == 0)
        def _():
            leg_z(0, asked_mid, wanted)

        for level in range(LEV):

            @pl.when(now == level)
            def _(level=level):
                level_end(level)

        @pl.when(now < NG)
        def _():
            spread_pair(now * 2 + 1)

        for late, stage in enumerate(stages):
            made = now - late
            double = jnp.logical_and(made >= READY, made < 2 * READY).astype(jnp.int32)
            single = jnp.logical_and(made >= 2 * READY, made < NG).astype(jnp.int32)
            begin = double * 2 * (made - READY) + single * made

            def run(group, carry, stage=stage):
                stage(group)
                return carry

            lax.fori_loop(begin, begin + 2 * double + single, run, 0)

        for stage in range(1, 4):

            @pl.when(now == LEV - 1 + stage)
            def _(stage=stage):
                gain_stage(stage)

        @pl.when(now == NG)
        def _():
            weight_copy.wait()

            def ghost_taps(number, carry):
                conv_taps(number * 3, 3, ROWS, GHOSTS)
                return carry

            lax.fori_loop(0, TAPS // 3, ghost_taps, 0)
            terms[...] = total[ROWS:, :].astype(bf16).reshape(4, 8, BUCKET, C)
            leg_x(4, terms, terms_mid)

        @pl.when(now == NG + 2)
        def _():
            leg_z(4, terms_mid, returned)

        @pl.when(now > NG)
        def _():
            def own_taps(number, carry):
                conv_taps(number * 3, 3, 0, ROWS)
                return carry

            begin = jnp.minimum((now - NG - 1) * 2, TAPS // 3)
            lax.fori_loop(begin, jnp.minimum(begin + 2, TAPS // 3), own_taps, 0)

        @pl.when(now == STEPS - 2)
        def _():
            leg_end(4, returned)
            back = returned[...].reshape(GHOSTS, C)
            term = pooled[...] * gainf[...]
            high = term.astype(bf16)
            rest = term - high.astype(f32)
            middle = rest.astype(bf16)
            low = (rest - middle.astype(f32)).astype(bf16)
            mask_rows = maskf[...]
            masks = jnp.concatenate([mask_rows, mask_rows, mask_rows], axis=0).T.astype(bf16)
            parts = jnp.concatenate([high.astype(f32), middle.astype(f32), low.astype(f32)], axis=0)
            for first in range(0, ROWS, 256):
                block = slice(first, first + 256)
                value = total[block, :] + jnp.dot(
                    owner_t[block, :], back, preferred_element_type=f32
                )
                value = value + jnp.dot(
                    masks[block, :], parts.astype(bf16), preferred_element_type=f32
                )
                fgrad_ref[block, :] = value.astype(bf16)

        return carry

    lax.fori_loop(0, STEPS, step, 0)

    wait_for(gains_z.at[0:7], gain_recv.at[3])
    gain_total = gains_z[0]
    for place in range(1, 8):
        gain_total = gain_total + gains_z[place]
    both = squares[...] + gain_total * gain_total
    norm2 = jnp.sum(jnp.sum(both, axis=1, keepdims=True), axis=0, keepdims=True) + tiny_eps
    factor = jnp.minimum(1.0, clip_norm / jnp.sqrt(norm2))
    gain_out[...] = gain_total * factor
    scale_out[...] = factor

    wait_for(wsum_ref, store_sem)
    wait_for(r0, send.at[0])
    wait_for(r1, send.at[1])
    wait_for(r2, send.at[2])
    wait_for(r3.at[:, 0:7], send.at[3])
    wait_for(r2, send.at[4])
    wait_for(r1, send.at[5])
    wait_for(a1, send.at[6])
    wait_for(asked_mid.at[0:3], halo_send.at[0])
    wait_for(wanted.at[:, 0:7], halo_send.at[1])
    for number in (2, 4):
        wait_for(ghosts.at[0:3], halo_send.at[number])
        wait_for(ghosts.at[:, 0:7], halo_send.at[number + 1])
    for level in range(LEV):
        wait_for(level_in.at[level], level_send.at[level])
    wait_for(gains0.at[0], gain_send.at[0])
    wait_for(gains_y.at[0:3], gain_send.at[1])
    wait_for(gains_x.at[0:3], gain_send.at[2])
    wait_for(gains_z.at[0:7], gain_send.at[3])


def on_device(features, grad_out, conv_weight, pool_gain, neighbours, requests, pool_mask):
    vmem = pl.BlockSpec(memory_space=pltpu.VMEM)
    dma = pltpu.SemaphoreType.DMA
    feature_grad, weight_sum, gain_grad, scale = pl.pallas_call(
        whole,
        out_shape=(
            jax.ShapeDtypeStruct((ROWS, C), bf16),
            jax.ShapeDtypeStruct((NG * R, C), bf16),
            jax.ShapeDtypeStruct((8, C), f32),
            jax.ShapeDtypeStruct((1, 1), f32),
        ),
        in_specs=[vmem] * 6 + [pl.BlockSpec(memory_space=pl.ANY)],
        out_specs=(vmem, pl.BlockSpec(memory_space=pl.ANY), vmem, vmem),
        scratch_shapes=[
            pltpu.VMEM((NG * R, C), bf16),
            pltpu.VMEM((TAPS, SLOTS, C), bf16),
            pltpu.VMEM((C, SLOTS), bf16),
            pltpu.VMEM((NG * R, C), f32),
            pltpu.VMEM((NG, HALF, C), f32),
            pltpu.VMEM((NG, HALF, C), bf16),
            pltpu.VMEM((NG, 3, QUARTER, C), bf16),
            pltpu.VMEM((NG, QUARTER, C), bf16),
            pltpu.VMEM((NG, 3, PIECE, C), bf16),
            pltpu.VMEM((NG, 8, PIECE, C), bf16),
            pltpu.VMEM((TAPS, C, C), bf16),
            pltpu.VMEM((SLOTS, C), f32),
            pltpu.VMEM((4, 8, 1, 128), jnp.int32),
            pltpu.VMEM((4, 8, 1, 128), jnp.int32),
            pltpu.VMEM((4, 8, 1, 128), jnp.int32),
            pltpu.VMEM((ROWS, GHOSTS), bf16),
            pltpu.VMEM((4, 8, BUCKET, C), bf16),
            pltpu.VMEM((4, 8, BUCKET, C), bf16),
            pltpu.VMEM((4, 8, BUCKET, C), bf16),
            pltpu.VMEM((4, 8, BUCKET, C), bf16),
            pltpu.VMEM((4, 8, BUCKET, C), bf16),
            pltpu.VMEM((4, 8, BUCKET, C), bf16),
            pltpu.VMEM((8, ROWS), f32),
            pltpu.VMEM((8, C), f32),
            pltpu.VMEM((LEV, 8, C), f32),
            pltpu.VMEM((LEV, 8, C), f32),
            pltpu.VMEM((8, C), f32),
            pltpu.VMEM((2, 8, C), f32),
            pltpu.VMEM((4, 8, C), f32),
            pltpu.VMEM((4, 8, C), f32),
            pltpu.VMEM((8, 8, C), f32),
            pltpu.VMEM((8, C), f32),
            dma((7,)),
            dma((7, NG)),
            dma((6,)),
            dma((6,)),
            dma((LEV,)),
            dma((LEV,)),
            dma((4,)),
            dma((4,)),
            dma,
            dma,
        ],
        compiler_params=pltpu.CompilerParams(
            collective_id=0, has_side_effects=True, vmem_limit_bytes=58 * 2**20
        ),
    )(features, grad_out, neighbours, requests.T, pool_mask, pool_gain, conv_weight)
    weight_sum = weight_sum[: TAPS * C].reshape(TAPS, C, C)
    return (feature_grad, weight_sum.astype(f32) * scale[0, 0], gain_grad[:LEV])


def solution(mesh):
    placed = (
        P(("row", "col"), None),
        P(("row", "col"), None),
        P(),
        P(),
        P(None, ("row", "col")),
        P(("row", "col"), None),
        P(None, ("row", "col")),
    )
    return jax.shard_map(
        on_device,
        mesh=mesh,
        in_specs=placed,
        out_specs=(P(("row", "col"), None), P(), P()),
        check_vma=False,
    )
```

```python
import jax
import jax.numpy as jnp
from jax import lax
from jax.experimental import pallas as pl
from jax.experimental.pallas import tpu as pltpu
from jax.sharding import PartitionSpec as P

MESH = pl.DeviceIdType.MESH
clip_norm = 1024.0
tiny_eps = 1e-06
ROWS = 1024
C = 256
TAPS = 27
BUCKET = 16
PEERS = 32
GHOSTS = PEERS * BUCKET
SLOTS = ROWS + GHOSTS
LEV = 5
T = 4
NG = 28 // T
R = T * C
HALF = R // 2
QUARTER = HALF // 4
PIECE = HALF // 16
READY = 2
STEPS = NG + 7
f32 = jnp.float32
bf16 = jnp.bfloat16


def wait_for(ref, sem):
    pltpu.make_async_copy(ref, ref, sem).wait()


def whole(
    features_ref,
    grad_ref,
    neighbours_ref,
    requests_ref,
    mask_ref,
    gain_ref,
    weight_hbm,
    fgrad_ref,
    wsum_hbm,
    gain_out,
    scale_out,
    wsum_ref,
    spread,
    ext_t,
    wpart,
    r0,
    a1,
    r1,
    a2,
    r2,
    r3,
    weight,
    total,
    asked,
    wanted,
    owner_t,
    outgoing,
    ghosts,
    terms,
    returned,
    maskf,
    gainf,
    level_out,
    level_in,
    pooled,
    gains0,
    gains_y,
    gains_x,
    gains_z,
    squares,
    send,
    recv,
    halo_send,
    halo_recv,
    level_send,
    level_recv,
    gain_send,
    gain_recv,
    weight_sem,
    store_sem,
):
    row = lax.axis_index("row")
    col = lax.axis_index("col")
    y = row // 2
    core = row % 2
    x = col // 8
    z = col % 8
    y_others = [(y + offset) % 4 for offset in range(1, 4)]
    x_others = [(x + offset) % 4 for offset in range(1, 4)]
    z_others = [(z + offset) % 8 for offset in range(1, 8)]
    y_rows = [other * 2 + core for other in y_others]
    x_cols = [other * 8 + z for other in x_others]
    z_cols = [x * 8 + other for other in z_others]
    other_core = (y * 2 + 1 - core, col)
    y_peers = [(there, col) for there in y_rows]
    x_peers = [(row, there) for there in x_cols]
    z_peers = [(row, there) for there in z_cols]
    across_cols = [there * 8 + other for there in x_others for other in z_others]
    across = [(row, there) for there in across_cols]
    near = y_peers + x_peers + z_peers + across + [other_core]

    def push(src, dst, send_sem, recv_sem, device):
        pltpu.make_async_remote_copy(
            src_ref=src,
            dst_ref=dst,
            send_sem=send_sem,
            recv_sem=recv_sem,
            device_id=device,
            device_id_type=MESH,
        ).start()

    weight_copy = pltpu.make_async_copy(weight_hbm, weight, weight_sem)
    weight_copy.start()

    barrier = pltpu.get_barrier_semaphore()
    for device in near:
        pl.semaphore_signal(barrier, inc=1, device_id=device, device_id_type=MESH)

    maskf[...] = jnp.zeros_like(maskf)
    maskf[0:LEV, :] = mask_ref[...].astype(f32)
    gainf[...] = jnp.zeros_like(gainf)
    gainf[0:LEV, :] = gain_ref[...]
    level_out[0] = jnp.dot(maskf[...].astype(bf16), grad_ref[...], preferred_element_type=f32)
    square = jnp.concatenate([requests_ref[...], jnp.zeros((128 - BUCKET, PEERS), jnp.int32)], axis=0)
    lists = square.astype(f32).T.astype(jnp.int32)
    for peer in range(PEERS):
        asked[peer] = lists[peer : peer + 1, :]
    wpart[TAPS * C :, :] = jnp.zeros(((NG * T - TAPS) * C, C), f32)
    squares[...] = jnp.zeros_like(squares)
    total[...] = jnp.zeros_like(total)
    ext_t[:, 0:ROWS] = features_ref[...].T

    pl.semaphore_wait(barrier, len(near))

    def exchange(number, src, dst):
        for peer in z_cols + x_cols + across_cols:
            push(src.at[peer], dst.at[col], halo_send.at[number], halo_recv.at[number], (row, peer))
        dst[pl.ds(col, 1)] = src[pl.ds(col, 1)]

    def arrived(number, dst, sems):
        wait_for(dst.at[0 : PEERS - 1], sems.at[number])

    exchange(0, asked, wanted)

    level_partner = (
        ((y + 2) % 4 * 2 + core, col),
        ((y + 1 - 2 * (y % 2)) * 2 + core, col),
        (y * 2 + 1 - core, col),
        (row, (x + 2) % 4 * 8 + z),
        (row, (x + 1 - 2 * (x % 2)) * 8 + z),
    )

    def level_start(level):
        push(
            level_out.at[level],
            level_in.at[level],
            level_send.at[level],
            level_recv.at[level],
            level_partner[level],
        )

    level_rows = lax.broadcasted_iota(jnp.int32, (8, C), 0)

    def level_end(level):
        wait_for(level_in.at[level], level_recv.at[level])
        summed = level_out[level] + jnp.where(level_rows >= level, level_in[level], 0.0)
        if level < LEV - 1:
            level_out[level + 1] = summed
            level_start(level + 1)
            return
        scale = jnp.zeros((8, C), f32)
        for row_level in range(LEV):
            value = (2.0 ** (row_level + 1) * ROWS) ** (-0.5)
            scale = jnp.where(level_rows == row_level, value, scale)
        pooled[...] = summed * scale
        feature_sums = jnp.dot(
            maskf[...].astype(bf16), features_ref[...], preferred_element_type=f32
        )
        gains0[0] = feature_sums * pooled[...]
        push(
            gains0.at[0], gains0.at[1], gain_send.at[0], gain_recv.at[0], other_core
        )

    def gain_stage(stage):
        if stage == 1:
            wait_for(gains0.at[1], gain_recv.at[0])
            gains_y[pl.ds(y, 1)] = (gains0[0] + gains0[1])[None]
            for device in y_peers:
                push(gains_y.at[y], gains_y.at[y], gain_send.at[1], gain_recv.at[1], device)
        elif stage == 2:
            wait_for(gains_y.at[0:3], gain_recv.at[1])
            gains_x[pl.ds(x, 1)] = jnp.sum(gains_y[...], axis=0, keepdims=True)
            for device in x_peers:
                push(gains_x.at[x], gains_x.at[x], gain_send.at[2], gain_recv.at[2], device)
        else:
            wait_for(gains_x.at[0:3], gain_recv.at[2])
            gains_z[pl.ds(z, 1)] = jnp.sum(gains_x[...], axis=0, keepdims=True)
            for device in z_peers:
                push(gains_z.at[z], gains_z.at[z], gain_send.at[3], gain_recv.at[3], device)

    level_start(0)

    def each_pair(group, body):
        def pair(number, carry):
            body(number * 2, 2)
            return carry

        lax.fori_loop(group * (T // 2), jnp.minimum((group + 1) * (T // 2), TAPS // 2), pair, 0)

        @pl.when(group == NG - 1)
        def _():
            body(TAPS - 1, 1)

    def spread_pair(pair):
        def body(begin, count):
            for late in range(count):
                index = neighbours_ref[pl.ds(begin + late, 1), :]
                for first in range(0, SLOTS, 256):
                    places = lax.broadcasted_iota(jnp.int16, (256, ROWS), 0)
                    hit = places == (index - first).astype(jnp.int16)
                    chosen = jnp.where(hit, bf16(1), bf16(0))
                    part = jnp.dot(chosen, grad_ref[...], preferred_element_type=f32)
                    spread[begin + late, first : first + 256, :] = part.astype(bf16)

        @pl.when(pair < TAPS // 2)
        def _():
            body(pair * 2, 2)

        @pl.when(pair == TAPS // 2)
        def _():
            body(TAPS - 1, 1)

    def weight_taps(group):
        def body(begin, count):
            for late in range(count):
                tap = begin + late
                wpart[pl.ds(pl.multiple_of(tap * C, C), C), :] = jnp.dot(
                    ext_t[...], spread[tap], preferred_element_type=f32
                )

        each_pair(group, body)

    def give_features():
        arrived(0, wanted, halo_recv)
        lists = jnp.broadcast_to(wanted[...].reshape(PEERS, 1, 128), (PEERS, BUCKET, 128)).reshape(GHOSTS, 128)
        lanes = lax.broadcasted_iota(jnp.int32, (GHOSTS, 128), 1)
        places = lax.broadcasted_iota(jnp.int32, (GHOSTS, 128), 0) % BUCKET
        picked = jnp.where(lanes == places, lists.astype(f32), 0.0)
        octant = jnp.sum(picked, axis=1, keepdims=True).astype(jnp.int32)
        octants = lax.broadcasted_iota(jnp.int32, (GHOSTS, ROWS), 1)
        chosen = jnp.where(octants == octant, 1.0, 0.0).astype(bf16)
        taken = jnp.dot(chosen, features_ref[...], preferred_element_type=f32).astype(bf16)
        outgoing[...] = taken.reshape(PEERS, BUCKET, C)
        exchange(1, outgoing, ghosts)
        owner_t[...] = chosen.T

    def order_of(group):
        odd = (group + group // 4) % 2
        return odd, y + (x - y) * odd, x + (y - x) * odd

    def peers_of(odd):
        chips = [b_ + (a_ - b_) * odd for a_, b_ in zip(x_others, y_others)]
        rows = [there + (row - there) * odd for there in y_rows]
        cols = [col + (there - col) * odd for there in x_cols]
        return zip(chips, zip(rows, cols))

    def rows_of(start, size):
        return pl.ds(pl.multiple_of(start, PIECE), size)

    def stage0(group):
        weight_taps(group)
        base = group * R
        push(
            wpart.at[rows_of(base + (1 - core) * HALF, HALF)],
            r0.at[group],
            send.at[0],
            recv.at[0, group],
            other_core,
        )

    def stage1(group):
        odd, first, second = order_of(group)
        wait_for(r0.at[group], recv.at[0, group])
        mine = rows_of(group * R + core * HALF, HALF)
        a1[group] = (wpart[mine, :] + r0[group]).astype(bf16)
        for place, (other, device) in enumerate(peers_of(odd)):
            push(
                a1.at[group, rows_of(other * QUARTER, QUARTER)],
                r1.at[group, place],
                send.at[1],
                recv.at[1, group],
                device,
            )

    def stage2(group):
        odd, first, second = order_of(group)
        wait_for(r1.at[group], recv.at[1, group])
        mine = rows_of(group * R + core * HALF + first * QUARTER, QUARTER)
        kept = wpart[mine, :] + r0[group, rows_of(first * QUARTER, QUARTER), :]
        for offset in range(3):
            kept = kept + r1[group, offset].astype(f32)
        a2[group] = kept.astype(bf16)
        for place, (other, device) in enumerate(peers_of(1 - odd)):
            push(
                a2.at[group, rows_of(other * PIECE, PIECE)],
                r2.at[group, place],
                send.at[2],
                recv.at[2, group],
                device,
            )

    def stage3(group):
        odd, first, second = order_of(group)
        wait_for(r2.at[group], recv.at[2, group])
        kept = a2[group, rows_of(second * PIECE, PIECE), :].astype(f32)
        for offset in range(3):
            kept = kept + r2[group, offset].astype(f32)
        r3[group, pl.ds(z, 1)] = kept.astype(bf16)[None]
        for device in z_peers:
            push(
                r3.at[group, z],
                r3.at[group, z],
                send.at[3],
                recv.at[3, group],
                device,
            )

    def stage4(group):
        odd, first, second = order_of(group)
        wait_for(r3.at[group, 0:7], recv.at[3, group])
        kept = r3[group, 0].astype(f32)
        for place in range(1, 8):
            kept = kept + r3[group, place].astype(f32)
        mine = rows_of(group * R + core * HALF + first * QUARTER + second * PIECE, PIECE)
        wsum_ref[mine, :] = kept.astype(bf16)
        for place, (other, device) in enumerate(peers_of(1 - odd)):
            push(
                wsum_ref.at[mine],
                wsum_ref.at[mine],
                send.at[4],
                recv.at[4, group],
                device,
            )

    def stage5(group):
        odd, first, second = order_of(group)
        wait_for(r2.at[group], recv.at[4, group])
        mine = rows_of(group * R + core * HALF + first * QUARTER, QUARTER)
        for place, (other, device) in enumerate(peers_of(odd)):
            push(
                wsum_ref.at[mine],
                wsum_ref.at[mine],
                send.at[5],
                recv.at[5, group],
                device,
            )

    def stage6(group):
        wait_for(r1.at[group], recv.at[5, group])
        mine = rows_of(group * R + core * HALF, HALF)
        push(
            wsum_ref.at[mine],
            wsum_ref.at[mine],
            send.at[6],
            recv.at[6, group],
            other_core,
        )

    def stage7(group):
        wait_for(a1.at[group], recv.at[6, group])

        def chunk(part, carry):
            value = wsum_ref[rows_of(group * R + part * 64, 64), :].astype(f32)
            squares[...] += jnp.sum((value * value).reshape(8, 8, C), axis=0)
            return carry

        done = rows_of(group * R, R)
        pltpu.make_async_copy(wsum_ref.at[done], wsum_hbm.at[done], store_sem).start()
        lax.fori_loop(0, R // 64, chunk, 0)

    stages = (stage0, stage1, stage2, stage3, stage4, stage5, stage6, stage7)

    def conv_taps(begin, count, start, size):
        value = total[start : start + size, :]
        for late in range(count):
            value = value + lax.dot_general(
                spread[begin + late, start : start + size, :],
                weight[begin + late],
                (((1,), (1,)), ((), ())),
                preferred_element_type=f32,
            )
        total[start : start + size, :] = value

    def step(now, carry):
        @pl.when(now == READY)
        def _():
            arrived(1, ghosts, halo_recv)
            ext_t[:, ROWS:] = ghosts[...].reshape(GHOSTS, C).T

        @pl.when(now < NG)
        def _():
            spread_pair(now * 2)

        @pl.when(now == 0)
        def _():
            give_features()

        for level in range(LEV):

            @pl.when(now == level + 1)
            def _(level=level):
                level_end(level)

        @pl.when(now < NG)
        def _():
            spread_pair(now * 2 + 1)

        for late, stage in enumerate(stages):
            made = now - late
            double = jnp.logical_and(made >= READY, made < 2 * READY).astype(jnp.int32)
            single = jnp.logical_and(made >= 2 * READY, made < NG).astype(jnp.int32)
            begin = double * 2 * (made - READY) + single * made

            def run(group, carry, stage=stage):
                stage(group)
                return carry

            lax.fori_loop(begin, begin + 2 * double + single, run, 0)

        for stage in range(1, 4):

            @pl.when(now == LEV + stage)
            def _(stage=stage):
                gain_stage(stage)

        @pl.when(now == NG)
        def _():
            weight_copy.wait()

            def ghost_taps(number, carry):
                conv_taps(number * 3, 3, ROWS, GHOSTS)
                return carry

            lax.fori_loop(0, TAPS // 3, ghost_taps, 0)
            terms[...] = total[ROWS:, :].astype(bf16).reshape(PEERS, BUCKET, C)
            exchange(2, terms, returned)

        @pl.when(now > NG)
        def _():
            def own_taps(number, carry):
                conv_taps(number * 3, 3, 0, ROWS)
                return carry

            begin = jnp.minimum((now - NG - 1) * 2, TAPS // 3)
            lax.fori_loop(begin, jnp.minimum(begin + 2, TAPS // 3), own_taps, 0)

        @pl.when(now == STEPS - 2)
        def _():
            arrived(2, returned, halo_recv)
            back = returned[...].reshape(GHOSTS, C)
            term = pooled[...] * gainf[...]
            high = term.astype(bf16)
            rest = term - high.astype(f32)
            middle = rest.astype(bf16)
            low = (rest - middle.astype(f32)).astype(bf16)
            mask_rows = maskf[...]
            masks = jnp.concatenate([mask_rows, mask_rows, mask_rows], axis=0).T.astype(bf16)
            parts = jnp.concatenate([high.astype(f32), middle.astype(f32), low.astype(f32)], axis=0)
            for first in range(0, ROWS, 256):
                block = slice(first, first + 256)
                value = total[block, :] + jnp.dot(
                    owner_t[block, :], back, preferred_element_type=f32
                )
                value = value + jnp.dot(
                    masks[block, :], parts.astype(bf16), preferred_element_type=f32
                )
                fgrad_ref[block, :] = value.astype(bf16)

        return carry

    lax.fori_loop(0, STEPS, step, 0)

    wait_for(gains_z.at[0:7], gain_recv.at[3])
    gain_total = gains_z[0]
    for place in range(1, 8):
        gain_total = gain_total + gains_z[place]
    both = squares[...] + gain_total * gain_total
    norm2 = jnp.sum(jnp.sum(both, axis=1, keepdims=True), axis=0, keepdims=True) + tiny_eps
    factor = jnp.minimum(1.0, clip_norm / jnp.sqrt(norm2))
    gain_out[...] = gain_total * factor
    scale_out[...] = factor

    wait_for(wsum_ref, store_sem)
    wait_for(r0, send.at[0])
    wait_for(r1, send.at[1])
    wait_for(r2, send.at[2])
    wait_for(r3.at[:, 0:7], send.at[3])
    wait_for(r2, send.at[4])
    wait_for(r1, send.at[5])
    wait_for(a1, send.at[6])
    arrived(0, wanted, halo_send)
    arrived(1, ghosts, halo_send)
    arrived(2, returned, halo_send)
    for level in range(LEV):
        wait_for(level_in.at[level], level_send.at[level])
    wait_for(gains0.at[0], gain_send.at[0])
    wait_for(gains_y.at[0:3], gain_send.at[1])
    wait_for(gains_x.at[0:3], gain_send.at[2])
    wait_for(gains_z.at[0:7], gain_send.at[3])


def scaled(scale_ref, sum_ref, gain_ref, fgrad_in, out_ref, gain_out, fgrad_out):
    here = pl.program_id(0)

    @pl.when(here == 0)
    def _():
        gain_out[...] = gain_ref[0:LEV, :]

    fgrad_out[...] = fgrad_in[...]
    out_ref[...] = sum_ref[...].astype(f32) * scale_ref[0, 0]


def on_device(features, grad_out, conv_weight, pool_gain, neighbours, requests, pool_mask):
    vmem = pl.BlockSpec(memory_space=pltpu.VMEM)
    dma = pltpu.SemaphoreType.DMA
    feature_grad, weight_sum, gain_grad, scale = pl.pallas_call(
        whole,
        out_shape=(
            jax.ShapeDtypeStruct((ROWS, C), bf16),
            jax.ShapeDtypeStruct((NG * R, C), bf16),
            jax.ShapeDtypeStruct((8, C), f32),
            jax.ShapeDtypeStruct((1, 1), f32),
        ),
        in_specs=[vmem] * 6 + [pl.BlockSpec(memory_space=pl.ANY)],
        out_specs=(vmem, pl.BlockSpec(memory_space=pl.ANY), vmem, vmem),
        scratch_shapes=[
            pltpu.VMEM((NG * R, C), bf16),
            pltpu.VMEM((TAPS, SLOTS, C), bf16),
            pltpu.VMEM((C, SLOTS), bf16),
            pltpu.VMEM((NG * R, C), f32),
            pltpu.VMEM((NG, HALF, C), f32),
            pltpu.VMEM((NG, HALF, C), bf16),
            pltpu.VMEM((NG, 3, QUARTER, C), bf16),
            pltpu.VMEM((NG, QUARTER, C), bf16),
            pltpu.VMEM((NG, 3, PIECE, C), bf16),
            pltpu.VMEM((NG, 8, PIECE, C), bf16),
            pltpu.VMEM((TAPS, C, C), bf16),
            pltpu.VMEM((SLOTS, C), f32),
            pltpu.VMEM((PEERS, 1, 128), jnp.int32),
            pltpu.VMEM((PEERS, 1, 128), jnp.int32),
            pltpu.VMEM((ROWS, GHOSTS), bf16),
            pltpu.VMEM((PEERS, BUCKET, C), bf16),
            pltpu.VMEM((PEERS, BUCKET, C), bf16),
            pltpu.VMEM((PEERS, BUCKET, C), bf16),
            pltpu.VMEM((PEERS, BUCKET, C), bf16),
            pltpu.VMEM((8, ROWS), f32),
            pltpu.VMEM((8, C), f32),
            pltpu.VMEM((LEV, 8, C), f32),
            pltpu.VMEM((LEV, 8, C), f32),
            pltpu.VMEM((8, C), f32),
            pltpu.VMEM((2, 8, C), f32),
            pltpu.VMEM((4, 8, C), f32),
            pltpu.VMEM((4, 8, C), f32),
            pltpu.VMEM((8, 8, C), f32),
            pltpu.VMEM((8, C), f32),
            dma((7,)),
            dma((7, NG)),
            dma((3,)),
            dma((3,)),
            dma((LEV,)),
            dma((LEV,)),
            dma((4,)),
            dma((4,)),
            dma,
            dma,
        ],
        compiler_params=pltpu.CompilerParams(
            collective_id=0, has_side_effects=True, vmem_limit_bytes=58 * 2**20
        ),
    )(features, grad_out, neighbours, requests.T, pool_mask, pool_gain, conv_weight)
    rows = 9 * C
    weight_grad, gain_grad, feature_grad = pl.pallas_call(
        scaled,
        grid=(TAPS * C // rows,),
        out_shape=(
            jax.ShapeDtypeStruct((TAPS * C, C), f32),
            jax.ShapeDtypeStruct((LEV, C), f32),
            jax.ShapeDtypeStruct((ROWS, C), bf16),
        ),
        in_specs=[
            pl.BlockSpec(memory_space=pltpu.SMEM),
            pl.BlockSpec((rows, C), lambda i: (i, 0)),
            pl.BlockSpec((8, C), lambda i: (0, 0)),
            pl.BlockSpec((ROWS, C), lambda i: (0, 0)),
        ],
        out_specs=(
            pl.BlockSpec((rows, C), lambda i: (i, 0)),
            pl.BlockSpec((LEV, C), lambda i: (0, 0)),
            pl.BlockSpec((ROWS, C), lambda i: (0, 0)),
        ),
        compiler_params=pltpu.CompilerParams(vmem_limit_bytes=60 * 2**20),
    )(scale, weight_sum, gain_grad, feature_grad)
    return (feature_grad, weight_grad.reshape(TAPS, C, C), gain_grad)


def solution(mesh):
    placed = (
        P(("row", "col"), None),
        P(("row", "col"), None),
        P(),
        P(),
        P(None, ("row", "col")),
        P(("row", "col"), None),
        P(None, ("row", "col")),
    )
    return jax.shard_map(
        on_device,
        mesh=mesh,
        in_specs=placed,
        out_specs=(P(("row", "col"), None), P(), P()),
        check_vma=False,
    )
```

```python
import jax
import jax.numpy as jnp
from jax import lax
from jax.experimental import pallas as pl
from jax.experimental.pallas import tpu as pltpu
from jax.sharding import PartitionSpec as P

MESH = pl.DeviceIdType.MESH
clip_norm = 1024.0
tiny_eps = 1e-06
ROWS = 1024
C = 256
TAPS = 27
BUCKET = 16
PEERS = 32
GHOSTS = PEERS * BUCKET
SLOTS = ROWS + GHOSTS
LEV = 5
T = 4
NG = 28 // T
R = T * C
HALF = R // 2
QUARTER = HALF // 4
PIECE = HALF // 16
READY = 2
STEPS = NG + 7
f32 = jnp.float32
bf16 = jnp.bfloat16


def wait_for(ref, sem):
    pltpu.make_async_copy(ref, ref, sem).wait()


def whole(
    features_ref,
    grad_ref,
    neighbours_ref,
    requests_ref,
    mask_ref,
    gain_ref,
    weight_hbm,
    fgrad_ref,
    wsum_hbm,
    gain_out,
    scale_out,
    wsum_ref,
    spread,
    ext_t,
    wpart,
    r0,
    a1,
    r1,
    a2,
    r2,
    r3,
    weight,
    total,
    asked,
    wanted,
    owner,
    owner_t,
    outgoing,
    ghosts,
    terms,
    returned,
    maskf,
    gainf,
    level_out,
    level_in,
    pooled,
    gains0,
    gains_y,
    gains_x,
    gains_z,
    squares,
    send,
    recv,
    halo_send,
    halo_recv,
    level_send,
    level_recv,
    gain_send,
    gain_recv,
    weight_sem,
    store_sem,
):
    row = lax.axis_index("row")
    col = lax.axis_index("col")
    y = row // 2
    core = row % 2
    x = col // 8
    z = col % 8
    y_others = [(y + offset) % 4 for offset in range(1, 4)]
    x_others = [(x + offset) % 4 for offset in range(1, 4)]
    z_others = [(z + offset) % 8 for offset in range(1, 8)]
    y_rows = [other * 2 + core for other in y_others]
    x_cols = [other * 8 + z for other in x_others]
    z_cols = [x * 8 + other for other in z_others]
    other_core = (y * 2 + 1 - core, col)
    y_peers = [(there, col) for there in y_rows]
    x_peers = [(row, there) for there in x_cols]
    z_peers = [(row, there) for there in z_cols]
    across_cols = [there * 8 + other for there in x_others for other in z_others]
    across = [(row, there) for there in across_cols]
    near = y_peers + x_peers + z_peers + across + [other_core]

    def push(src, dst, send_sem, recv_sem, device):
        pltpu.make_async_remote_copy(
            src_ref=src,
            dst_ref=dst,
            send_sem=send_sem,
            recv_sem=recv_sem,
            device_id=device,
            device_id_type=MESH,
        ).start()

    weight_copy = pltpu.make_async_copy(weight_hbm, weight, weight_sem)
    weight_copy.start()

    barrier = pltpu.get_barrier_semaphore()
    for device in near:
        pl.semaphore_signal(barrier, inc=1, device_id=device, device_id_type=MESH)

    maskf[...] = jnp.zeros_like(maskf)
    maskf[0:LEV, :] = mask_ref[...].astype(f32)
    gainf[...] = jnp.zeros_like(gainf)
    gainf[0:LEV, :] = gain_ref[...]
    level_out[0] = jnp.dot(maskf[...].astype(bf16), grad_ref[...], preferred_element_type=f32)
    square = jnp.concatenate([requests_ref[...], jnp.zeros((128 - BUCKET, PEERS), jnp.int32)], axis=0)
    lists = square.astype(f32).T.astype(jnp.int32)
    for peer in range(PEERS):
        asked[peer] = lists[peer : peer + 1, :]
    wpart[TAPS * C :, :] = jnp.zeros(((NG * T - TAPS) * C, C), f32)
    squares[...] = jnp.zeros_like(squares)
    total[...] = jnp.zeros_like(total)
    ext_t[:, 0:ROWS] = features_ref[...].T

    pl.semaphore_wait(barrier, len(near))

    def exchange(number, src, dst):
        for peer in z_cols + x_cols + across_cols:
            push(src.at[peer], dst.at[col], halo_send.at[number], halo_recv.at[number], (row, peer))
        dst[pl.ds(col, 1)] = src[pl.ds(col, 1)]

    def arrived(number, dst, sems):
        wait_for(dst.at[0 : PEERS - 1], sems.at[number])

    exchange(0, asked, wanted)

    level_partner = (
        ((y + 2) % 4 * 2 + core, col),
        ((y + 1 - 2 * (y % 2)) * 2 + core, col),
        (y * 2 + 1 - core, col),
        (row, (x + 2) % 4 * 8 + z),
        (row, (x + 1 - 2 * (x % 2)) * 8 + z),
    )

    def level_start(level):
        push(
            level_out.at[level],
            level_in.at[level],
            level_send.at[level],
            level_recv.at[level],
            level_partner[level],
        )

    level_rows = lax.broadcasted_iota(jnp.int32, (8, C), 0)

    def level_end(level):
        wait_for(level_in.at[level], level_recv.at[level])
        summed = level_out[level] + jnp.where(level_rows >= level, level_in[level], 0.0)
        if level < LEV - 1:
            level_out[level + 1] = summed
            level_start(level + 1)
            return
        scale = jnp.zeros((8, C), f32)
        for row_level in range(LEV):
            value = (2.0 ** (row_level + 1) * ROWS) ** (-0.5)
            scale = jnp.where(level_rows == row_level, value, scale)
        pooled[...] = summed * scale
        feature_sums = jnp.dot(
            maskf[...].astype(bf16), features_ref[...], preferred_element_type=f32
        )
        gains0[0] = feature_sums * pooled[...]
        push(
            gains0.at[0], gains0.at[1], gain_send.at[0], gain_recv.at[0], other_core
        )

    def gain_stage(stage):
        if stage == 1:
            wait_for(gains0.at[1], gain_recv.at[0])
            gains_y[pl.ds(y, 1)] = (gains0[0] + gains0[1])[None]
            for device in y_peers:
                push(gains_y.at[y], gains_y.at[y], gain_send.at[1], gain_recv.at[1], device)
        elif stage == 2:
            wait_for(gains_y.at[0:3], gain_recv.at[1])
            gains_x[pl.ds(x, 1)] = jnp.sum(gains_y[...], axis=0, keepdims=True)
            for device in x_peers:
                push(gains_x.at[x], gains_x.at[x], gain_send.at[2], gain_recv.at[2], device)
        else:
            wait_for(gains_x.at[0:3], gain_recv.at[2])
            gains_z[pl.ds(z, 1)] = jnp.sum(gains_x[...], axis=0, keepdims=True)
            for device in z_peers:
                push(gains_z.at[z], gains_z.at[z], gain_send.at[3], gain_recv.at[3], device)

    level_start(0)

    def each_pair(group, body):
        def pair(number, carry):
            body(number * 2, 2)
            return carry

        lax.fori_loop(group * (T // 2), jnp.minimum((group + 1) * (T // 2), TAPS // 2), pair, 0)

        @pl.when(group == NG - 1)
        def _():
            body(TAPS - 1, 1)

    def spread_pair(pair):
        def body(begin, count):
            for late in range(count):
                index = neighbours_ref[pl.ds(begin + late, 1), :]
                for first in range(0, SLOTS, 256):
                    places = lax.broadcasted_iota(jnp.int16, (256, ROWS), 0)
                    hit = places == (index - first).astype(jnp.int16)
                    chosen = jnp.where(hit, bf16(1), bf16(0))
                    part = jnp.dot(chosen, grad_ref[...], preferred_element_type=f32)
                    spread[begin + late, first : first + 256, :] = part.astype(bf16)

        @pl.when(pair < TAPS // 2)
        def _():
            body(pair * 2, 2)

        @pl.when(pair == TAPS // 2)
        def _():
            body(TAPS - 1, 1)

    def weight_taps(group):
        def body(begin, count):
            for late in range(count):
                tap = begin + late
                wpart[pl.ds(pl.multiple_of(tap * C, C), C), :] = jnp.dot(
                    ext_t[...], spread[tap], preferred_element_type=f32
                )

        each_pair(group, body)

    def give_features():
        arrived(0, wanted, halo_recv)
        lists = jnp.broadcast_to(wanted[...].reshape(PEERS, 1, 128), (PEERS, BUCKET, 128)).reshape(GHOSTS, 128)
        lanes = lax.broadcasted_iota(jnp.int32, (GHOSTS, 128), 1)
        places = lax.broadcasted_iota(jnp.int32, (GHOSTS, 128), 0) % BUCKET
        picked = jnp.where(lanes == places, lists.astype(f32), 0.0)
        octant = jnp.sum(picked, axis=1, keepdims=True).astype(jnp.int32)
        octants = lax.broadcasted_iota(jnp.int32, (GHOSTS, ROWS), 1)
        chosen = jnp.where(octants == octant, 1.0, 0.0).astype(bf16)
        taken = jnp.dot(chosen, features_ref[...], preferred_element_type=f32).astype(bf16)
        outgoing[...] = taken.reshape(PEERS, BUCKET, C)
        exchange(1, outgoing, ghosts)
        owner[...] = chosen

    def order_of(group):
        odd = (group + group // 4) % 2
        return odd, y + (x - y) * odd, x + (y - x) * odd

    def peers_of(odd):
        chips = [b_ + (a_ - b_) * odd for a_, b_ in zip(x_others, y_others)]
        rows = [there + (row - there) * odd for there in y_rows]
        cols = [col + (there - col) * odd for there in x_cols]
        return zip(chips, zip(rows, cols))

    def rows_of(start, size):
        return pl.ds(pl.multiple_of(start, PIECE), size)

    def stage0(group):
        weight_taps(group)
        base = group * R
        push(
            wpart.at[rows_of(base + (1 - core) * HALF, HALF)],
            r0.at[group],
            send.at[0],
            recv.at[0, group],
            other_core,
        )

    def stage1(group):
        odd, first, second = order_of(group)
        wait_for(r0.at[group], recv.at[0, group])
        mine = rows_of(group * R + core * HALF, HALF)
        a1[group] = (wpart[mine, :] + r0[group]).astype(bf16)
        for place, (other, device) in enumerate(peers_of(odd)):
            push(
                a1.at[group, rows_of(other * QUARTER, QUARTER)],
                r1.at[group, place],
                send.at[1],
                recv.at[1, group],
                device,
            )

    def stage2(group):
        odd, first, second = order_of(group)
        wait_for(r1.at[group], recv.at[1, group])
        mine = rows_of(group * R + core * HALF + first * QUARTER, QUARTER)
        kept = wpart[mine, :] + r0[group, rows_of(first * QUARTER, QUARTER), :]
        for offset in range(3):
            kept = kept + r1[group, offset].astype(f32)
        a2[group] = kept.astype(bf16)
        for place, (other, device) in enumerate(peers_of(1 - odd)):
            push(
                a2.at[group, rows_of(other * PIECE, PIECE)],
                r2.at[group, place],
                send.at[2],
                recv.at[2, group],
                device,
            )

    def stage3(group):
        odd, first, second = order_of(group)
        wait_for(r2.at[group], recv.at[2, group])
        kept = a2[group, rows_of(second * PIECE, PIECE), :].astype(f32)
        for offset in range(3):
            kept = kept + r2[group, offset].astype(f32)
        r3[group, pl.ds(z, 1)] = kept.astype(bf16)[None]
        for device in z_peers:
            push(
                r3.at[group, z],
                r3.at[group, z],
                send.at[3],
                recv.at[3, group],
                device,
            )

    def stage4(group):
        odd, first, second = order_of(group)
        wait_for(r3.at[group, 0:7], recv.at[3, group])
        kept = r3[group, 0].astype(f32)
        for place in range(1, 8):
            kept = kept + r3[group, place].astype(f32)
        mine = rows_of(group * R + core * HALF + first * QUARTER + second * PIECE, PIECE)
        wsum_ref[mine, :] = kept.astype(bf16)
        for place, (other, device) in enumerate(peers_of(1 - odd)):
            push(
                wsum_ref.at[mine],
                wsum_ref.at[mine],
                send.at[4],
                recv.at[4, group],
                device,
            )

    def stage5(group):
        odd, first, second = order_of(group)
        wait_for(r2.at[group], recv.at[4, group])
        mine = rows_of(group * R + core * HALF + first * QUARTER, QUARTER)
        for place, (other, device) in enumerate(peers_of(odd)):
            push(
                wsum_ref.at[mine],
                wsum_ref.at[mine],
                send.at[5],
                recv.at[5, group],
                device,
            )

    def stage6(group):
        wait_for(r1.at[group], recv.at[5, group])
        mine = rows_of(group * R + core * HALF, HALF)
        push(
            wsum_ref.at[mine],
            wsum_ref.at[mine],
            send.at[6],
            recv.at[6, group],
            other_core,
        )

    def stage7(group):
        wait_for(a1.at[group], recv.at[6, group])

        def chunk(part, carry):
            value = wsum_ref[rows_of(group * R + part * 64, 64), :].astype(f32)
            squares[...] += jnp.sum((value * value).reshape(8, 8, C), axis=0)
            return carry

        done = rows_of(group * R, R)
        pltpu.make_async_copy(wsum_ref.at[done], wsum_hbm.at[done], store_sem).start()
        lax.fori_loop(0, R // 64, chunk, 0)

    stages = (stage0, stage1, stage2, stage3, stage4, stage5, stage6, stage7)

    def conv_taps(begin, count, start, size):
        value = total[start : start + size, :]
        for late in range(count):
            value = value + lax.dot_general(
                spread[begin + late, start : start + size, :],
                weight[begin + late],
                (((1,), (1,)), ((), ())),
                preferred_element_type=f32,
            )
        total[start : start + size, :] = value

    def step(now, carry):
        @pl.when(now == READY)
        def _():
            arrived(1, ghosts, halo_recv)
            ext_t[:, ROWS:] = ghosts[...].reshape(GHOSTS, C).T

        @pl.when(now < NG)
        def _():
            spread_pair(now * 2)

        @pl.when(now == 0)
        def _():
            give_features()

        for level in range(LEV):

            @pl.when(now == level + 1)
            def _(level=level):
                level_end(level)

        @pl.when(now < NG)
        def _():
            spread_pair(now * 2 + 1)

        for late, stage in enumerate(stages):
            made = now - late
            double = jnp.logical_and(made >= READY, made < 2 * READY).astype(jnp.int32)
            single = jnp.logical_and(made >= 2 * READY, made < NG).astype(jnp.int32)
            begin = double * 2 * (made - READY) + single * made

            def run(group, carry, stage=stage):
                stage(group)
                return carry

            lax.fori_loop(begin, begin + 2 * double + single, run, 0)

        for stage in range(1, 4):

            @pl.when(now == LEV + stage)
            def _(stage=stage):
                gain_stage(stage)

        @pl.when(now == NG)
        def _():
            weight_copy.wait()

            def ghost_taps(number, carry):
                conv_taps(number * 3, 3, ROWS, GHOSTS)
                return carry

            lax.fori_loop(0, TAPS // 3, ghost_taps, 0)
            terms[...] = total[ROWS:, :].astype(bf16).reshape(PEERS, BUCKET, C)
            exchange(2, terms, returned)

        @pl.when(now == NG + 3)
        def _():
            owner_t[...] = owner[...].T

        @pl.when(now > NG)
        def _():
            def own_taps(number, carry):
                conv_taps(number * 3, 3, 0, ROWS)
                return carry

            begin = jnp.minimum((now - NG - 1) * 2, TAPS // 3)
            lax.fori_loop(begin, jnp.minimum(begin + 2, TAPS // 3), own_taps, 0)

        @pl.when(now == STEPS - 2)
        def _():
            arrived(2, returned, halo_recv)
            back = returned[...].reshape(GHOSTS, C)
            term = pooled[...] * gainf[...]
            high = term.astype(bf16)
            rest = term - high.astype(f32)
            middle = rest.astype(bf16)
            low = (rest - middle.astype(f32)).astype(bf16)
            mask_rows = maskf[...]
            masks = jnp.concatenate([mask_rows, mask_rows, mask_rows], axis=0).T.astype(bf16)
            parts = jnp.concatenate([high.astype(f32), middle.astype(f32), low.astype(f32)], axis=0)
            for first in range(0, ROWS, 256):
                block = slice(first, first + 256)
                value = total[block, :] + jnp.dot(
                    owner_t[block, :], back, preferred_element_type=f32
                )
                value = value + jnp.dot(
                    masks[block, :], parts.astype(bf16), preferred_element_type=f32
                )
                fgrad_ref[block, :] = value.astype(bf16)

        return carry

    lax.fori_loop(0, STEPS, step, 0)

    wait_for(gains_z.at[0:7], gain_recv.at[3])
    gain_total = gains_z[0]
    for place in range(1, 8):
        gain_total = gain_total + gains_z[place]
    both = squares[...] + gain_total * gain_total
    norm2 = jnp.sum(jnp.sum(both, axis=1, keepdims=True), axis=0, keepdims=True) + tiny_eps
    factor = jnp.minimum(1.0, clip_norm / jnp.sqrt(norm2))
    gain_out[...] = gain_total * factor
    scale_out[...] = factor

    wait_for(wsum_ref, store_sem)
    wait_for(r0, send.at[0])
    wait_for(r1, send.at[1])
    wait_for(r2, send.at[2])
    wait_for(r3.at[:, 0:7], send.at[3])
    wait_for(r2, send.at[4])
    wait_for(r1, send.at[5])
    wait_for(a1, send.at[6])
    arrived(0, wanted, halo_send)
    arrived(1, ghosts, halo_send)
    arrived(2, returned, halo_send)
    for level in range(LEV):
        wait_for(level_in.at[level], level_send.at[level])
    wait_for(gains0.at[0], gain_send.at[0])
    wait_for(gains_y.at[0:3], gain_send.at[1])
    wait_for(gains_x.at[0:3], gain_send.at[2])
    wait_for(gains_z.at[0:7], gain_send.at[3])


def scaled(scale_ref, sum_ref, gain_ref, fgrad_in, out_ref, gain_out, fgrad_out):
    here = pl.program_id(0)

    @pl.when(here == 0)
    def _():
        gain_out[...] = gain_ref[0:LEV, :]

    fgrad_out[...] = fgrad_in[...]
    out_ref[...] = sum_ref[...].astype(f32) * scale_ref[0, 0]


def on_device(features, grad_out, conv_weight, pool_gain, neighbours, requests, pool_mask):
    vmem = pl.BlockSpec(memory_space=pltpu.VMEM)
    dma = pltpu.SemaphoreType.DMA
    feature_grad, weight_sum, gain_grad, scale = pl.pallas_call(
        whole,
        out_shape=(
            jax.ShapeDtypeStruct((ROWS, C), bf16),
            jax.ShapeDtypeStruct((NG * R, C), bf16),
            jax.ShapeDtypeStruct((8, C), f32),
            jax.ShapeDtypeStruct((1, 1), f32),
        ),
        in_specs=[vmem] * 6 + [pl.BlockSpec(memory_space=pl.ANY)],
        out_specs=(vmem, pl.BlockSpec(memory_space=pl.ANY), vmem, vmem),
        scratch_shapes=[
            pltpu.VMEM((NG * R, C), bf16),
            pltpu.VMEM((TAPS, SLOTS, C), bf16),
            pltpu.VMEM((C, SLOTS), bf16),
            pltpu.VMEM((NG * R, C), f32),
            pltpu.VMEM((NG, HALF, C), f32),
            pltpu.VMEM((NG, HALF, C), bf16),
            pltpu.VMEM((NG, 3, QUARTER, C), bf16),
            pltpu.VMEM((NG, QUARTER, C), bf16),
            pltpu.VMEM((NG, 3, PIECE, C), bf16),
            pltpu.VMEM((NG, 8, PIECE, C), bf16),
            pltpu.VMEM((TAPS, C, C), bf16),
            pltpu.VMEM((SLOTS, C), f32),
            pltpu.VMEM((PEERS, 1, 128), jnp.int32),
            pltpu.VMEM((PEERS, 1, 128), jnp.int32),
            pltpu.VMEM((GHOSTS, ROWS), bf16),
            pltpu.VMEM((ROWS, GHOSTS), bf16),
            pltpu.VMEM((PEERS, BUCKET, C), bf16),
            pltpu.VMEM((PEERS, BUCKET, C), bf16),
            pltpu.VMEM((PEERS, BUCKET, C), bf16),
            pltpu.VMEM((PEERS, BUCKET, C), bf16),
            pltpu.VMEM((8, ROWS), f32),
            pltpu.VMEM((8, C), f32),
            pltpu.VMEM((LEV, 8, C), f32),
            pltpu.VMEM((LEV, 8, C), f32),
            pltpu.VMEM((8, C), f32),
            pltpu.VMEM((2, 8, C), f32),
            pltpu.VMEM((4, 8, C), f32),
            pltpu.VMEM((4, 8, C), f32),
            pltpu.VMEM((8, 8, C), f32),
            pltpu.VMEM((8, C), f32),
            dma((7,)),
            dma((7, NG)),
            dma((3,)),
            dma((3,)),
            dma((LEV,)),
            dma((LEV,)),
            dma((4,)),
            dma((4,)),
            dma,
            dma,
        ],
        compiler_params=pltpu.CompilerParams(
            collective_id=0, has_side_effects=True, vmem_limit_bytes=58 * 2**20
        ),
    )(features, grad_out, neighbours, requests.T, pool_mask, pool_gain, conv_weight)
    rows = 9 * C
    weight_grad, gain_grad, feature_grad = pl.pallas_call(
        scaled,
        grid=(TAPS * C // rows,),
        out_shape=(
            jax.ShapeDtypeStruct((TAPS * C, C), f32),
            jax.ShapeDtypeStruct((LEV, C), f32),
            jax.ShapeDtypeStruct((ROWS, C), bf16),
        ),
        in_specs=[
            pl.BlockSpec(memory_space=pltpu.SMEM),
            pl.BlockSpec((rows, C), lambda i: (i, 0)),
            pl.BlockSpec((8, C), lambda i: (0, 0)),
            pl.BlockSpec((ROWS, C), lambda i: (0, 0)),
        ],
        out_specs=(
            pl.BlockSpec((rows, C), lambda i: (i, 0)),
            pl.BlockSpec((LEV, C), lambda i: (0, 0)),
            pl.BlockSpec((ROWS, C), lambda i: (0, 0)),
        ),
        compiler_params=pltpu.CompilerParams(vmem_limit_bytes=60 * 2**20),
    )(scale, weight_sum, gain_grad, feature_grad)
    return (feature_grad, weight_grad.reshape(TAPS, C, C), gain_grad)


def solution(mesh):
    placed = (
        P(("row", "col"), None),
        P(("row", "col"), None),
        P(),
        P(),
        P(None, ("row", "col")),
        P(("row", "col"), None),
        P(None, ("row", "col")),
    )
    return jax.shard_map(
        on_device,
        mesh=mesh,
        in_specs=placed,
        out_specs=(P(("row", "col"), None), P(), P()),
        check_vma=False,
    )
```
